32 devices in a mesh: groups: 2 (over y), seq: 4 (over z), head: 2 (over x), rep: 2 (over core).
Axes of the slice: x: 2, y: 2, z: 4, core: 2. Of those that a mesh axis runs over, the one named last changes fastest.
Arguments:
- queries: bfloat16 [16384, 2048], P(('groups', 'seq'), ('head', 'rep')), parts along dimension 0, may hold values from -4.5 to 4.5
- key_rows: bfloat16 [16384, 256], P(('groups', 'seq'), 'head'), parts along dimension 0, may hold values from -4.5 to 4.5
- value_rows: bfloat16 [16384, 256], P(('groups', 'seq'), 'head'), parts along dimension 0, may hold values from -8 to 8
- vertical_columns: int32 [4, 1024], P('groups'), parts along dimension 0, may hold values from 0 to 8191, as said below
- slash_offsets: int32 [4, 8], P('groups'), parts along dimension 0, may hold values from 0 to 3968, as said below
Outputs:
- attended: bfloat16 [16384, 2048], P(('groups', 'seq'), ('head', 'rep')), parts along dimension 0
- log_norm: float32 [16, 16384], P(('head', 'rep'), ('groups', 'seq')), parts along dimension 1
The draws below stay inside these ranges and needn't reach their ends.
There are 2 independent parts, one for each index of `groups`. The reference program is written for one: setup_inputs(seed, part) draws one part's arguments, and reference() takes and returns one part's arrays. A program takes and returns all parts, laid end to end along the dimension named above; each array names one. Nothing has to cross between parts.
Inputs may be any that keep to these rules, and one draw needn't show every extreme that they name: `vertical_columns`: each row lists 1024 distinct positions in rising order; each aligned block of 2048 positions holds at most 384 entries of a row, and the first block holds exactly 384. `slash_offsets`: each row lists 8 distinct multiples of 128 in rising order, always including 0 and (31) * 128.
All inputs are finite; a program needn't handle non-finite values.
Results may differ from the reference program's by a relative error of at most 0.0033.
Values may be sent and summed in bfloat16 or wider, within the bound.
No kernel may reach another device: no remote copies, remote signals or barrier semaphores. Data moves between devices by JAX's collectives and lax.ppermute only.
A program may use at most 64 MiB of HBM per device.

```python
import math
import jax
import jax.numpy as jnp
from jax import lax

GQ = 8
HD = 128
BLK = 128
SPAN = 32
NVERT = 1024
NSLASH = 8
S_DEV = 2048
TOKENS = 8192
KVH = 2
QH = 16
VMAX = 384


def draw_queries(key, part):
    key = jax.random.fold_in(key, 1)
    filled = jnp.clip(1.5 * jax.random.normal(key, (TOKENS, QH * HD), jnp.float32), -4.5, 4.5)
    return filled.astype(jnp.bfloat16)


def draw_key_rows(key, part):
    key = jax.random.fold_in(key, 2)
    filled = jnp.clip(1.5 * jax.random.normal(key, (TOKENS, KVH * HD), jnp.float32), -4.5, 4.5)
    return filled.astype(jnp.bfloat16)


def draw_vertical_columns(key, part):
    key = jax.random.fold_in(key, 7)
    shard_total = TOKENS // S_DEV

    def shard_order(order_key):
        return jax.random.permutation(order_key, S_DEV)

    def one_head(head_key):
        first_key, slot_key, place_key = jax.random.split(head_key, 3)
        opening = jax.random.permutation(first_key, S_DEV)[:VMAX]
        slots = jax.random.permutation(slot_key, (shard_total - 1) * VMAX)[:NVERT - VMAX]
        shard_ids = 1 + slots // VMAX
        orders = jax.vmap(shard_order)(jax.random.split(place_key, shard_total - 1))
        placed = orders[shard_ids - 1, slots % VMAX] + shard_ids * S_DEV
        return jnp.sort(jnp.concatenate([opening, placed]).astype(jnp.int32))
    return jax.vmap(one_head)(jax.random.split(key, KVH)).astype(jnp.int32)


def draw_slash_offsets(key, part):
    key = jax.random.fold_in(key, 5)

    def one_head(head_key):
        middle = jax.random.permutation(head_key, SPAN - 2)[:NSLASH - 2] + 1
        listed = jnp.concatenate([jnp.zeros((1,), jnp.int32), middle.astype(jnp.int32), jnp.full((1,), SPAN - 1, jnp.int32)])
        return jnp.sort(listed) * BLK
    return jax.vmap(one_head)(jax.random.split(key, KVH)).astype(jnp.int32)


def shard_levels(stream_key, shape, cuts, least, high):
    factor_of, own = 1.0, jax.random.fold_in(stream_key, 6)
    for axis_at, parts in cuts:
        heights = jnp.exp(jax.random.uniform(jax.random.fold_in(own, axis_at), (parts,), jnp.float32, least / len(cuts), high / len(cuts)))
        factor_of = factor_of * jnp.repeat(heights, shape[axis_at] // parts).reshape([-1 if axis == axis_at else 1 for axis in range(len(shape))])
    return factor_of


def centred(own_key, shape, deviation, most, shards=(), held_as=jnp.bfloat16):
    entries = jax.random.normal(own_key, shape, jnp.float32) * deviation
    if len(shards) > 0:
        entries = shard_levels(own_key, shape, shards, -0.22, 0.18) * entries
    return jnp.clip(entries, min=-most, max=most).astype(held_as)


def setup_inputs(seed: int = 0, part: int = 0) -> dict:
    key_of = jax.random.split(jax.random.key(seed), 6)
    part_keys = jax.random.split(jax.random.fold_in(key_of[5], part), 6)
    return {
        "queries": draw_queries(jax.random.fold_in(jax.random.fold_in(key_of[5], part), 71), part),
        "key_rows": draw_key_rows(jax.random.fold_in(jax.random.fold_in(key_of[5], part), 71), part),
        "value_rows": centred(part_keys[2], (TOKENS, KVH * HD), 2.0, 8.0, ((0, 4), (1, 2))),
        "vertical_columns": draw_vertical_columns(jax.random.fold_in(jax.random.fold_in(key_of[5], part), 71), part),
        "slash_offsets": draw_slash_offsets(jax.random.fold_in(jax.random.fold_in(key_of[5], part), 71), part),
    }


def reference(queries, key_rows, value_rows, vertical_columns, slash_offsets):
    tokens = queries.shape[0]
    nblocks = tokens // BLK
    scale = 1.0 / math.sqrt(HD)
    offsets_in = jnp.arange(BLK, dtype=jnp.int32)

    def per_head(head_id):
        keys_here = lax.dynamic_slice_in_dim(key_rows, head_id * HD, HD, 1)
        values_here = lax.dynamic_slice_in_dim(value_rows, head_id * HD, HD, 1)
        columns = lax.dynamic_index_in_dim(vertical_columns, head_id, 0, keepdims=False)
        shifts = lax.dynamic_index_in_dim(slash_offsets, head_id, 0, keepdims=False) // BLK
        vert_keys = jnp.take(keys_here, columns, axis=0)
        vert_values = jnp.take(values_here, columns, axis=0)
        key_blocks = keys_here.reshape(nblocks, BLK, HD)
        value_blocks = values_here.reshape(nblocks, BLK, HD)
        query_here = lax.dynamic_slice_in_dim(queries, head_id * GQ * HD, GQ * HD, 1).reshape(nblocks, BLK, GQ, HD)

        def per_block(block_id):
            source = block_id - shifts
            tile_valid = source >= 0
            source = jnp.maximum(source, 0)
            slash_keys = jnp.take(key_blocks, source, axis=0).reshape(-1, HD)
            slash_values = jnp.take(value_blocks, source, axis=0).reshape(-1, HD)
            all_keys = jnp.concatenate([slash_keys, vert_keys], axis=0).astype(jnp.float32)
            all_values = jnp.concatenate([slash_values, vert_values], axis=0).astype(jnp.float32)
            query_block = lax.dynamic_index_in_dim(query_here, block_id, 0, keepdims=False).astype(jnp.float32)
            scores = jnp.einsum('rgd,kd->grk', query_block, all_keys) * scale
            query_pos = block_id * BLK + offsets_in
            slash_mask = (tile_valid[None, :, None] & ((shifts[None, :, None] > 0) | (offsets_in[None, None, :] <= offsets_in[:, None, None]))).reshape(BLK, -1)
            distance = block_id - columns // BLK
            banned = jnp.any(distance[:, None] == shifts[None, :], axis=1)
            vert_mask = (columns[None, :] <= query_pos[:, None]) & jnp.logical_not(banned)[None, :]
            visible = jnp.concatenate([slash_mask, vert_mask], axis=1)
            masked = jnp.where(visible[None], scores, -1e+30)
            row_peak = lax.optimization_barrier(jnp.max(masked, axis=-1))
            weights = jnp.where(visible[None], jnp.exp(masked - row_peak[..., None]), 0.0)
            row_total = lax.optimization_barrier(jnp.sum(weights, axis=-1))
            rounded = weights.astype(jnp.bfloat16).astype(jnp.float32)
            weighted = jnp.einsum('grk,kd->grd', rounded, all_values) / row_total[..., None]
            return (jnp.transpose(weighted.astype(jnp.bfloat16), (1, 0, 2)), row_peak + jnp.log(row_total))
        return lax.map(per_block, jnp.arange(nblocks, dtype=jnp.int32))
    outputs, log_parts = lax.map(per_head, jnp.arange(KVH, dtype=jnp.int32))
    attended = jnp.transpose(outputs, (1, 2, 0, 3, 4)).reshape(tokens, KVH * GQ * HD)
    log_norm = jnp.transpose(log_parts, (0, 2, 1, 3)).reshape(KVH * GQ, tokens)
    return (attended, log_norm)
```

```python
import functools
import math

import jax
import jax.numpy as jnp
from jax import lax
from jax.experimental import pallas as pl
from jax.experimental.pallas import tpu as pltpu
from jax.sharding import PartitionSpec as P

BLK = 128
SPAN = 32
LANES = 128
NEG = -1e30
LIMIT = 1e30
LN2 = math.log(2.0)
VMEM_BYTES = 60 * 1024 * 1024
BF16 = jnp.bfloat16
F32 = jnp.float32


def shifted(value, axis, steps):
    count = lax.axis_size(axis)
    leading, last = (max(0, -steps), min(count, count - steps))
    return lax.ppermute(value, axis, [(source, source + steps) for source in range(leading, last)])


def swapped(value):
    return lax.ppermute(value, "rep", [(0, 1), (1, 0)])


def dot(left, right, left_dim, right_dim):
    return lax.dot_general(
        left, right, (((left_dim,), (right_dim,)), ((), ())), preferred_element_type=F32
    )


def sublane_sums(values):
    return jnp.sum(values.reshape(-1, 8, values.shape[1]), axis=0)


def pack_kernel(meta, positions, *refs):
    *parts, out = refs
    slots = positions.shape[0]
    total = jnp.zeros((slots, 2 * LANES), F32)
    where = positions[...]
    row0 = 0
    for mine, other in zip(parts[0::2], parts[1::2]):
        for start in range(0, mine.shape[0], 512):
            hot = jnp.concatenate(
                [
                    jnp.where(
                        where
                        == lax.broadcasted_iota(jnp.int32, where.shape, 1)
                        + (row0 + start + lane0),
                        1.0,
                        0.0,
                    ).astype(BF16)
                    for lane0 in range(0, 512, LANES)
                ],
                axis=1,
            )
            rows = jnp.concatenate(
                [mine[start : start + 512, :], other[start : start + 512, :]], axis=1
            )
            total = total + dot(hot, rows, 1, 0)
        row0 += mine.shape[0]
    packed = total.astype(BF16)
    first, second = packed[:, :LANES], packed[:, LANES:]

    @pl.when(meta[0] == 0)
    def _():
        out[...] = jnp.concatenate([first, second], axis=1)

    @pl.when(meta[0] != 0)
    def _():
        out[...] = jnp.concatenate([second, first], axis=1)


def pack(order, positions, parts):
    slots = positions.shape[0]
    flat = [array for pair in parts for array in pair]
    return pl.pallas_call(
        pack_kernel,
        grid_spec=pltpu.PrefetchScalarGridSpec(
            num_scalar_prefetch=1,
            grid=(1,),
            in_specs=[
                pl.BlockSpec(array.shape, lambda step, meta: (0, 0))
                for array in [positions] + flat
            ],
            out_specs=pl.BlockSpec((slots, 2 * LANES), lambda step, meta: (0, 0)),
        ),
        out_shape=jax.ShapeDtypeStruct((slots, 2 * LANES), BF16),
        compiler_params=pltpu.CompilerParams(vmem_limit_bytes=VMEM_BYTES),
        cost_estimate=pl.CostEstimate(
            flops=2 * slots * 2048 * 256, bytes_accessed=1 << 20, transcendentals=0
        ),
        name="pack_rows",
    )(order, positions, *flat)


def stage_kernel(cfg, meta, q_ref, *refs):
    refs = list(refs)
    nslash = cfg["nslash"]
    heads = q_ref.shape[1] // LANES
    width = heads * BLK
    per_step = cfg["per_step"]
    factor = cfg["factor"]
    first, last = cfg["first"], cfg["last"]
    groups = cfg["groups"]
    sources = cfg["sources"]
    step = pl.program_id(0)
    block0 = meta[nslash]
    core = meta[nslash + 1]

    if not first:
        acc_in, stat_in = refs.pop(0), refs.pop(0)
    vert_refs = [(refs.pop(0), refs.pop(0)) for _ in groups]
    source_refs = [(refs.pop(0), refs.pop(0)) for _ in sources]
    spare_refs = [(refs.pop(0), refs.pop(0)) for _ in cfg["spare"]]
    out_a, out_b = refs.pop(0), refs.pop(0)
    kx, vx, sems = refs.pop(0), refs.pop(0), refs.pop(0)
    if last:
        redo_k, redo_e, redo_acc, redo_stat, redo_sems = refs

    def source_copies(swap):
        copies = []
        for place, ((row0, rows, fixed), (mine, other)) in enumerate(zip(sources, source_refs)):
            targets = (vx, kx) if swap and not fixed else (kx, vx)
            for which, (ref, target) in enumerate(zip((mine, other), targets)):
                copies.append(
                    pltpu.make_async_copy(
                        ref, target.at[pl.ds(row0, rows), :], sems.at[2 * place + which]
                    )
                )
        return copies

    @pl.when(step == 0)
    def _():
        @pl.when(core == 0)
        def _():
            for copy in source_copies(False):
                copy.start()

        @pl.when(core != 0)
        def _():
            for copy in source_copies(True):
                copy.start()

        for copy in source_copies(False):
            copy.wait()

    def tile_rows(index):
        return pl.ds(pl.multiple_of(index * BLK, BLK), BLK)

    def slash_tile(block, place):
        shift = meta[place]
        bias = jnp.where(block0 + block - shift >= 0, 0.0, NEG).astype(F32)
        return jnp.maximum(cfg["own_tile"] + block - shift, 0), bias

    def query_rows(unit):
        rows = slice(unit * BLK, (unit + 1) * BLK)
        return jnp.concatenate(
            [q_ref[rows, h * LANES : (h + 1) * LANES] for h in range(heads)], axis=0
        )

    def marked(query, block):
        lane = lax.broadcasted_iota(jnp.int32, (query.shape[0], LANES), 1)
        return jnp.concatenate([query, jnp.where(lane == block, 1.0, 0.0).astype(BF16)], axis=1)

    def causal(scores):
        key_at = lax.broadcasted_iota(jnp.int32, scores.shape, 0)
        query_at = lax.broadcasted_iota(jnp.int32, scores.shape, 1) % BLK
        return jnp.where(key_at <= query_at, scores, NEG)

    def finish(unit, acc, sums, peak):
        total = jnp.sum(sums, axis=0, keepdims=True)
        result = (acc / total).astype(BF16)
        norm = peak[:1] * LN2 + jnp.log(total)
        for h in range(heads):
            part = slice(h * LANES, (h + 1) * LANES)
            out_a[unit * BLK : (unit + 1) * BLK, part] = result[:, part].T
            out_b[h : h + 1, unit * BLK : (unit + 1) * BLK] = norm[:, part]
        return total

    def one_unit(unit, tiles, with_slash):
        block = step * per_step + unit
        query = query_rows(unit)
        rows = slice(unit * BLK, (unit + 1) * BLK)
        stat = 2 * 8 * unit
        acc = sums = None
        if first:
            own = tile_rows(cfg["own_tile"] + block)
            scores = causal(dot(kx[own, :], query, 1, 1)) * factor
            peak = jnp.broadcast_to(jnp.max(scores, axis=0, keepdims=True), (8, width))
            weights = jnp.exp2(scores - peak[:1])
            sums = sublane_sums(weights)
            acc = dot(vx[own, :], weights.astype(BF16), 0, 0)
        else:
            sums = stat_in[stat : stat + 8, :]
            peak = stat_in[stat + 8 : stat + 16, :]
        base = peak[:1]
        if sum(tiles):
            keys = jnp.concatenate(
                [
                    jnp.concatenate([kv[: n * BLK, :LANES], mark[: n * BLK, :]], axis=1)
                    for n, (kv, mark) in zip(tiles, vert_refs)
                    if n
                ],
                axis=0,
            )
            values = jnp.concatenate(
                [kv[: n * BLK, LANES:] for n, (kv, _) in zip(tiles, vert_refs) if n], axis=0
            )
            weights = jnp.exp2(dot(keys, marked(query, block), 1, 1) * factor - base)
            sums = sums + sublane_sums(weights)
            more = dot(values, weights.astype(BF16), 0, 0)
            acc = more if acc is None else acc + more
        if with_slash:
            chosen = [slash_tile(block, place) for place in range(1, nslash)]
            keys = jnp.concatenate([kx[tile_rows(index), :] for index, _ in chosen], axis=0)
            values = jnp.concatenate([vx[tile_rows(index), :] for index, _ in chosen], axis=0)
            scores = dot(keys, query, 1, 1)
            parts = []
            for place, (_, bias) in enumerate(chosen):
                weights = jnp.exp2(
                    scores[place * BLK : (place + 1) * BLK, :] * factor + (bias - base)
                )
                sums = sums + sublane_sums(weights)
                parts.append(weights.astype(BF16))
            more = dot(values, jnp.concatenate(parts, axis=0), 0, 0)
            acc = more if acc is None else acc + more
        if not first:
            acc = acc_in[rows, :] if acc is None else acc_in[rows, :] + acc
        if last:
            return finish(unit, acc, sums, peak)
        out_a[rows, :] = acc
        out_b[stat : stat + 8, :] = sums
        out_b[stat + 8 : stat + 16, :] = peak
        return None

    def redo(unit):
        block = step * per_step + unit
        query = query_rows(unit)
        copies = []
        row0 = 0
        for place, (kv, mark) in enumerate(spare_refs):
            part = pl.ds(row0, kv.shape[0])
            copies.append(pltpu.make_async_copy(kv, redo_k.at[part, :], redo_sems.at[2 * place]))
            copies.append(
                pltpu.make_async_copy(mark, redo_e.at[part, :], redo_sems.at[2 * place + 1])
            )
            row0 += kv.shape[0]
        for copy in copies:
            copy.start()
        for copy in copies:
            copy.wait()
        redo_acc[...] = jnp.zeros_like(redo_acc)
        redo_stat[0:8, :] = jnp.zeros((8, width), F32)
        redo_stat[8:16, :] = jnp.full((8, width), NEG, F32)

        def merge(scores, values):
            peak = redo_stat[8:16, :]
            high = jnp.maximum(peak, jnp.max(scores, axis=0, keepdims=True))
            weights = jnp.where(scores > 1e-3 * NEG, jnp.exp2(scores - high[:1]), 0.0)
            shrink = jnp.exp2(peak - high)
            redo_stat[0:8, :] = redo_stat[0:8, :] * shrink + sublane_sums(weights)
            redo_stat[8:16, :] = high
            redo_acc[...] = redo_acc[...] * shrink[:1] + dot(values, weights.astype(BF16), 0, 0)

        def slash_step(place, carry):
            index, bias = slash_tile(block, place)
            scores = dot(kx[tile_rows(index), :], query, 1, 1) * factor + bias
            key_at = lax.broadcasted_iota(jnp.int32, scores.shape, 0)
            query_at = lax.broadcasted_iota(jnp.int32, scores.shape, 1) % BLK
            reach = jnp.where(meta[place] > 0, BLK, 0)
            merge(jnp.where(key_at <= query_at + reach, scores, NEG), vx[tile_rows(index), :])
            return carry

        def vert_step(tile, carry):
            here = tile_rows(tile)
            keys = jnp.concatenate([redo_k[here, :LANES], redo_e[here, :]], axis=1)
            merge(dot(keys, marked(query, block), 1, 1) * factor, redo_k[here, LANES:])
            return carry

        lax.fori_loop(0, nslash, slash_step, 0)
        lax.fori_loop(0, redo_k.shape[0] // BLK, vert_step, 0)
        finish(unit, redo_acc[...], redo_stat[0:8, :], redo_stat[8:16, :])

    def whole_step(tiles):
        totals = [one_unit(unit, tiles, cfg["slash"]) for unit in range(per_step)]
        if last:
            for unit, total in enumerate(totals):
                worst = jnp.max(jnp.where(total < LIMIT, 0.0, 1.0))

                @pl.when(worst > 0.0)
                def _():
                    redo(unit)

    small = [min(n, 2) for n in groups]
    limited = [g for g, n in enumerate(groups) if n > 2 and cfg["counted"][g]]
    if limited:
        fits = functools.reduce(
            jnp.logical_and, [meta[nslash + 2 + g] <= 2 * BLK for g in limited]
        )
        few = [small[g] if g in limited else n for g, n in enumerate(groups)]

        @pl.when(fits)
        def _():
            whole_step(few)

        @pl.when(jnp.logical_not(fits))
        def _():
            whole_step(groups)
    else:
        whole_step(groups)


def stage(meta, queries, state, verts, counted, sources, spare, *, nslash, first, last, slash, own_tile, tiles, per_step=2):
    rows, columns = queries.shape
    heads = columns // LANES
    width = heads * BLK
    nblocks = rows // BLK
    cfg = dict(
        nslash=nslash,
        per_step=per_step,
        factor=1.0 / (math.sqrt(LANES) * LN2),
        first=first,
        last=last,
        slash=slash,
        own_tile=own_tile,
        groups=[kv.shape[0] // BLK for kv, _ in verts],
        counted=counted,
        sources=[(row0, mine.shape[0], fixed) for row0, fixed, mine, _ in sources],
        spare=[kv.shape for kv, _ in spare],
    )

    def moving(block_rows):
        return pl.BlockSpec((block_rows * per_step, width), lambda step, meta: (step, 0))

    def whole(array):
        return pl.BlockSpec(array.shape, lambda step, meta: (0, 0))

    anywhere = pl.BlockSpec(memory_space=pl.ANY)
    operands, specs = [queries], [pl.BlockSpec((BLK * per_step, columns), lambda s, m: (s, 0))]
    if not first:
        operands += list(state)
        specs += [moving(BLK), moving(16)]
    for pair in verts:
        operands += list(pair)
        specs += [whole(array) for array in pair]
    for _, _, mine, other in sources:
        operands += [mine, other]
        specs += [anywhere, anywhere]
    for pair in spare:
        operands += list(pair)
        specs += [anywhere, anywhere]
    scratch = [
        pltpu.VMEM((tiles * BLK, LANES), BF16),
        pltpu.VMEM((tiles * BLK, LANES), BF16),
        pltpu.SemaphoreType.DMA((2 * len(sources),)),
    ]
    if last:
        out_shape = [
            jax.ShapeDtypeStruct((rows, columns), BF16),
            jax.ShapeDtypeStruct((heads, rows), F32),
        ]
        out_specs = [
            pl.BlockSpec((BLK * per_step, columns), lambda s, m: (s, 0)),
            pl.BlockSpec((heads, BLK * per_step), lambda s, m: (0, s)),
        ]
        spare_rows = sum(kv.shape[0] for kv, _ in spare)
        scratch += [
            pltpu.VMEM((spare_rows, 2 * LANES), BF16),
            pltpu.VMEM((spare_rows, LANES), BF16),
            pltpu.VMEM((BLK, width), F32),
            pltpu.VMEM((16, width), F32),
            pltpu.SemaphoreType.DMA((2 * len(spare),)),
        ]
    else:
        out_shape = [
            jax.ShapeDtypeStruct((nblocks * BLK, width), F32),
            jax.ShapeDtypeStruct((nblocks * 16, width), F32),
        ]
        out_specs = [moving(BLK), moving(16)]
    keys = sum(kv.shape[0] for kv, _ in verts) + (nslash - 1) * BLK * slash + BLK * first
    return pl.pallas_call(
        functools.partial(stage_kernel, cfg),
        grid_spec=pltpu.PrefetchScalarGridSpec(
            num_scalar_prefetch=1,
            grid=(nblocks // per_step,),
            in_specs=specs,
            out_specs=out_specs,
            scratch_shapes=scratch,
        ),
        out_shape=out_shape,
        compiler_params=pltpu.CompilerParams(vmem_limit_bytes=VMEM_BYTES),
        cost_estimate=pl.CostEstimate(
            flops=8 * rows * heads * keys * LANES,
            bytes_accessed=8 << 20,
            transcendentals=rows * heads * keys,
        ),
        name="attend_stage",
    )(meta, *operands)


def body(queries, key_rows, value_rows, vertical_columns, slash_offsets):
    seq_count = lax.axis_size("seq")
    seq_index = lax.axis_index("seq")
    head_index = lax.axis_index("head")
    core = lax.axis_index("rep")
    tok_rows = queries.shape[0]
    nblocks = tok_rows // BLK
    radius = (SPAN + nblocks - 2) // nblocks
    nvert = vertical_columns.shape[1]
    nslash = slash_offsets.shape[1]
    slot_count = 3 * nvert // (2 * seq_count)
    slot_pad = -(-slot_count // BLK) * BLK

    payload = jnp.where(core == 0, key_rows, value_rows)
    half = tok_rows // 2
    order = [1, 0]
    hops = [[None, None] for _ in range(radius)]
    for piece in order:
        moved = payload[piece * half : (piece + 1) * half]
        for hop in range(radius):
            moved = shifted(moved, "seq", 1)
            hops[hop][piece] = (moved, swapped(moved))

    columns = lax.dynamic_index_in_dim(vertical_columns, head_index, 0, keepdims=False)
    shifts = lax.dynamic_index_in_dim(slash_offsets, head_index, 0, keepdims=False) // BLK
    padded = jnp.concatenate([columns, jnp.full((slot_pad,), tok_rows * seq_count, jnp.int32)])
    own_blocks = seq_index * nblocks + jnp.arange(LANES, dtype=jnp.int32)

    def slots_of(distance, count):
        start = (seq_index - distance) * tok_rows
        ahead = jnp.sum((columns < start).astype(jnp.int32))
        listed = lax.dynamic_slice_in_dim(padded, ahead, count, 0)
        valid = (listed < start + tok_rows) & (start >= 0)
        return (listed, valid, jnp.where(valid, listed - start, -1))

    def marks_of(listed, valid):
        distance = own_blocks[None, :] - (listed // BLK)[:, None]
        seen = valid[:, None] & (distance > 0)
        for place in range(nslash):
            seen = seen & (distance != shifts[place])
        return jnp.where(seen, 0.0, NEG).astype(BF16)

    near = [slots_of(distance, slot_pad) for distance in range(radius + 1)]
    near_marks = [marks_of(listed, valid) for listed, valid, _ in near]
    near_places = [
        jnp.broadcast_to(place[:, None], (slot_pad, LANES)) for _, _, place in near
    ]
    counts = [jnp.sum(valid.astype(jnp.int32)) for _, valid, _ in near]

    none = jnp.zeros((1,), jnp.int32)
    core_meta = jnp.reshape(core, (1,)).astype(jnp.int32)
    own_pack = pack(none, near_places[0], [(key_rows, value_rows)])
    own_verts = (own_pack, near_marks[0])

    far_verts = []
    distances = list(range(radius + 1, seq_count))
    if distances:
        far_payload = jnp.where(
            core == 0, own_pack[:slot_count, :LANES], own_pack[:slot_count, LANES:]
        )
        rows, listed, valid = [], [], []
        for distance in distances:
            mine = shifted(far_payload, "seq", distance)
            other = swapped(mine)
            rows.append(
                jnp.where(
                    core == 0,
                    jnp.concatenate([mine, other], axis=1),
                    jnp.concatenate([other, mine], axis=1),
                )
            )
            at, ok, _ = slots_of(distance, slot_count)
            listed.append(at)
            valid.append(ok)
        extra = -len(distances) * slot_count % BLK
        far_rows = jnp.pad(jnp.concatenate(rows, axis=0), ((0, extra), (0, 0)))
        far_marks = marks_of(
            jnp.pad(jnp.concatenate(listed), (0, extra)),
            jnp.pad(jnp.concatenate(valid), (0, extra)),
        )
        far_verts = [(far_rows, far_marks)]

    base_meta = jnp.concatenate(
        [
            shifts.astype(jnp.int32),
            jnp.reshape(seq_index * nblocks, (1,)).astype(jnp.int32),
            core_meta,
        ]
    )
    meta = jnp.concatenate([base_meta] + [jnp.reshape(count, (1,)) for count in counts])

    own_source = [(0, True, key_rows, value_rows)]
    state = stage(
        meta[: nslash + 3], queries, None, [own_verts], [True], own_source, [],
        nslash=nslash, first=True, last=False, slash=False, own_tile=0, tiles=nblocks,
    )
    hop_verts = [
        (pack(core_meta, near_places[hop + 1], hops[hop]), near_marks[hop + 1])
        for hop in range(radius)
    ]
    sources = []
    for hop in range(radius):
        for piece in range(2):
            row0 = (radius - 1 - hop) * tok_rows + piece * half
            sources.append((row0, False) + hops[hop][piece])
    sources.append((radius * tok_rows, True, key_rows, value_rows))
    rest = hop_verts + far_verts
    return tuple(
        stage(
            jnp.concatenate([base_meta, meta[nslash + 3 :], jnp.zeros((1,), jnp.int32)]),
            queries, state, rest, [True] * radius + [False] * len(far_verts), sources,
            [own_verts] + rest,
            nslash=nslash, first=False, last=True, slash=True, own_tile=radius * nblocks,
            tiles=(radius + 1) * nblocks,
        )
    )


def solution(mesh):
    placed = (
        P(("groups", "seq"), ("head", "rep")),
        P(("groups", "seq"), "head"),
        P(("groups", "seq"), "head"),
        P("groups", None),
        P("groups", None),
    )
    return jax.shard_map(
        body,
        mesh=mesh,
        in_specs=placed,
        out_specs=(P(("groups", "seq"), ("head", "rep")), P(("head", "rep"), ("groups", "seq"))),
        check_vma=False,
    )
```

```python
import functools
import math

import jax
import jax.numpy as jnp
from jax import lax
from jax.experimental import pallas as pl
from jax.experimental.pallas import tpu as pltpu
from jax.sharding import PartitionSpec as P

BLK = 128
SPAN = 32
LANES = 128
NEG = -1e30
LIMIT = 1e30
LN2 = math.log(2.0)
VMEM_BYTES = 30 * 1024 * 1024
BF16 = jnp.bfloat16
F32 = jnp.float32


def shifted(value, axis, steps):
    count = lax.axis_size(axis)
    leading, last = (max(0, -steps), min(count, count - steps))
    return lax.ppermute(value, axis, [(source, source + steps) for source in range(leading, last)])


def swapped(value):
    return lax.ppermute(value, "rep", [(0, 1), (1, 0)])


def after(*values):
    return lax.optimization_barrier(values)


def dot(left, right, left_dim, right_dim):
    return lax.dot_general(
        left, right, (((left_dim,), (right_dim,)), ((), ())), preferred_element_type=F32
    )


def sublane_sums(values):
    return jnp.sum(values.reshape(-1, 8, values.shape[1]), axis=0)


def one_hot_rows(places, rows_of, count):
    total = jnp.zeros((places.shape[0], 2 * LANES), F32)
    for start in range(0, count, 512):
        hot = jnp.concatenate(
            [
                jnp.where(
                    places
                    == lax.broadcasted_iota(jnp.int32, places.shape, 1) + (start + lane0),
                    1.0,
                    0.0,
                ).astype(BF16)
                for lane0 in range(0, 512, LANES)
            ],
            axis=1,
        )
        total = total + dot(hot, rows_of(start, 512), 1, 0)
    return total.astype(BF16)


def prep_kernel(cfg, offsets, columns_ref, k_ref, v_ref, *refs):
    tok_rows, slot_pad, near = cfg["tok_rows"], cfg["slot_pad"], cfg["near"]
    marks, places, packed, counts = refs[: near + 1], refs[near + 1 : -2], refs[-2], refs[-1]
    seq_index = lax.axis_index("seq")
    head_index = lax.axis_index("head")
    nvert = columns_ref.shape[1]
    nblocks = tok_rows // BLK
    columns = columns_ref[pl.ds(head_index, 1), :]
    wide = jnp.broadcast_to(columns, (8, nvert))
    shifts = [offsets[head_index, place] // BLK for place in range(offsets.shape[1])]

    def ahead_of(start):
        return jnp.sum((columns < start).astype(jnp.int32))

    after = ahead_of((seq_index + 1) * tok_rows)
    for distance in range(cfg["seq_count"]):
        start = (seq_index - distance) * tok_rows
        ahead = ahead_of(start)
        turned = pltpu.roll(wide, lax.rem(nvert - ahead, nvert), 1)
        if distance < near:
            counts[distance] = after - ahead
        after = ahead
        for tile in range(slot_pad // BLK):
            part = slice(tile * BLK, (tile + 1) * BLK)
            listed = jnp.broadcast_to(turned[0:1, part], (BLK, BLK)).T
            inside = (listed >= start) & (listed < start + tok_rows) & (start >= 0)
            lane = lax.broadcasted_iota(jnp.int32, listed.shape, 1)
            gap = seq_index * nblocks + lane - lax.shift_right_arithmetic(listed, 7)
            seen = inside & (gap > 0)
            for shift in shifts:
                seen = seen & (gap != shift)
            where = slice(tile * BLK, (tile + 1) * BLK)
            if distance >= near:
                row0 = (distance - near) * slot_pad + tile * BLK
                where = slice(row0, row0 + BLK)
            marks[min(distance, near)][where, :] = jnp.where(seen, 0.0, NEG).astype(BF16)
            if distance < near:
                places[distance][where, :] = jnp.where(inside, listed - start, -1)
    packed[...] = one_hot_rows(
        places[0][...],
        lambda row0, rows: jnp.concatenate(
            [k_ref[row0 : row0 + rows, :], v_ref[row0 : row0 + rows, :]], axis=1
        ),
        tok_rows,
    )


def prep(offsets, columns, key_rows, value_rows, seq_count, near, slot_pad):
    def whole(shape):
        return pl.BlockSpec(shape, lambda step, offsets: (0, 0))

    far_rows = max(seq_count - near, 1) * slot_pad
    shapes = [(slot_pad, LANES)] * near + [(far_rows, LANES)]
    places = [(slot_pad, LANES)] * near
    return pl.pallas_call(
        functools.partial(
            prep_kernel,
            dict(tok_rows=key_rows.shape[0], slot_pad=slot_pad, near=near, seq_count=seq_count),
        ),
        grid_spec=pltpu.PrefetchScalarGridSpec(
            num_scalar_prefetch=1,
            grid=(1,),
            in_specs=[whole(a.shape) for a in (columns, key_rows, value_rows)],
            out_specs=[whole(shape) for shape in shapes + places + [(slot_pad, 2 * LANES)]]
            + [pl.BlockSpec(memory_space=pltpu.SMEM)],
        ),
        out_shape=[jax.ShapeDtypeStruct(shape, BF16) for shape in shapes]
        + [jax.ShapeDtypeStruct(shape, jnp.int32) for shape in places]
        + [
            jax.ShapeDtypeStruct((slot_pad, 2 * LANES), BF16),
            jax.ShapeDtypeStruct((8,), jnp.int32),
        ],
        compiler_params=pltpu.CompilerParams(vmem_limit_bytes=VMEM_BYTES),
        cost_estimate=pl.CostEstimate(flops=1 << 31, bytes_accessed=1 << 20, transcendentals=0),
        name="prepare",
    )(offsets, columns, key_rows, value_rows)


def stage_kernel(cfg, offsets, counts, q_ref, *refs):
    refs = list(refs)
    nslash = offsets.shape[1]
    heads = q_ref.shape[1] // LANES
    width = heads * BLK
    per_step = cfg["per_step"]
    factor = cfg["factor"]
    first, last = cfg["first"], cfg["last"]
    sources = cfg["sources"]
    step = pl.program_id(0)
    block_from = cfg["step_from"] * per_step + step * per_step
    block0 = lax.axis_index("seq") * cfg["nblocks"]
    core = lax.axis_index("rep")
    head_index = lax.axis_index("head")

    state_refs = [(refs.pop(0), refs.pop(0)) for _ in range(cfg["states"])]
    vert_refs = [[refs.pop(0), refs.pop(0)] for _ in cfg["groups"]]
    source_refs = [(refs.pop(0), refs.pop(0)) for _ in sources]
    spare_refs = [(refs.pop(0), refs.pop(0)) for _ in range(cfg["spares"])]
    out_a, out_b = refs.pop(0), refs.pop(0)
    pack_out = refs.pop(0) if cfg["packs"] and not last else None
    if sources:
        kx, vx, sems = refs.pop(0), refs.pop(0), refs.pop(0)
    if cfg["packs"]:
        pack_ref = refs.pop(0)
    if last:
        redo_k, redo_e, redo_acc, redo_stat, redo_sems = refs

    def source_copies(swap):
        copies = []
        for place, ((row0, rows, fixed), (mine, other)) in enumerate(zip(sources, source_refs)):
            targets = (vx, kx) if swap and not fixed else (kx, vx)
            for which, (ref, target) in enumerate(zip((mine, other), targets)):
                copies.append(
                    pltpu.make_async_copy(
                        ref, target.at[pl.ds(row0, rows), :], sems.at[2 * place + which]
                    )
                )
        return copies

    if sources:

        @pl.when(step == 0)
        def _():
            @pl.when(core == 0)
            def _():
                for copy in source_copies(False):
                    copy.start()

            @pl.when(core != 0)
            def _():
                for copy in source_copies(True):
                    copy.start()

            for copy in source_copies(False):
                copy.wait()
            if cfg["packs"]:
                row0 = cfg["pack_row0"]
                pack_ref[...] = one_hot_rows(
                    vert_refs[0][0][...],
                    lambda at, rows: jnp.concatenate(
                        [
                            kx[row0 + at : row0 + at + rows, :],
                            vx[row0 + at : row0 + at + rows, :],
                        ],
                        axis=1,
                    ),
                    cfg["tok_rows"],
                )
                if pack_out is not None:
                    pack_out[...] = pack_ref[...]

    if cfg["packs"]:
        vert_refs[0][0] = pack_ref

    def tile_rows(index):
        return pl.ds(pl.multiple_of(index * BLK, BLK), BLK)

    def slash_tile(block, place):
        shift = offsets[head_index, place] // BLK
        bias = jnp.where(block0 + block - shift >= 0, 0.0, NEG).astype(F32)
        return jnp.maximum(cfg["own_tile"] + block - shift, 0), bias

    def query_rows(unit):
        rows = slice(unit * BLK, (unit + 1) * BLK)
        return jnp.concatenate(
            [q_ref[rows, h * LANES : (h + 1) * LANES] for h in range(heads)], axis=0
        )

    def marked(query, block):
        lane = lax.broadcasted_iota(jnp.int32, (query.shape[0], LANES), 1)
        return jnp.concatenate([query, jnp.where(lane == block, 1.0, 0.0).astype(BF16)], axis=1)

    def finish(unit, acc, sums, peak):
        total = jnp.sum(sums, axis=0, keepdims=True)
        result = (acc * (1.0 / total)).astype(BF16)
        norm = peak[:1] * LN2 + jnp.log(total)
        for h in range(heads):
            part = slice(h * LANES, (h + 1) * LANES)
            out_a[unit * BLK : (unit + 1) * BLK, part] = result[:, part].T
            out_b[h : h + 1, unit * BLK : (unit + 1) * BLK] = norm[:, part]
        return total

    def one_unit(unit, tiles, with_slash, state):
        block = block_from + unit
        query = query_rows(unit)
        rows = slice(unit * BLK, (unit + 1) * BLK)
        stat = 2 * 8 * unit
        acc = sums = None
        if first:
            own = tile_rows(cfg["own_tile"] + block)
            scores = dot(kx[own, :], query, 1, 1)
            key_at = lax.broadcasted_iota(jnp.int32, scores.shape, 0)
            query_at = lax.broadcasted_iota(jnp.int32, scores.shape, 1) % BLK
            scores = jnp.where(key_at <= query_at, scores, NEG) * factor
            peak = jnp.broadcast_to(jnp.max(scores, axis=0, keepdims=True), (8, width))
            weights = jnp.exp2(scores - peak[:1]).astype(BF16)
            sums = sublane_sums(weights.astype(F32))
            acc = dot(vx[own, :], weights, 0, 0)
        else:
            acc_in, stat_in = state_refs[state]
            sums = stat_in[stat : stat + 8, :]
            peak = stat_in[stat + 8 : stat + 16, :]
        base = peak[:1]
        if sum(tiles):
            keys = jnp.concatenate(
                [
                    jnp.concatenate([kv[: n * BLK, :LANES], mark[: n * BLK, :]], axis=1)
                    for n, (kv, mark) in zip(tiles, vert_refs)
                    if n
                ],
                axis=0,
            )
            values = jnp.concatenate(
                [kv[: n * BLK, LANES:] for n, (kv, _) in zip(tiles, vert_refs) if n], axis=0
            )
            weights = jnp.exp2(dot(keys, marked(query, block), 1, 1) * factor - base).astype(BF16)
            sums = sums + sublane_sums(weights.astype(F32))
            more = dot(values, weights, 0, 0)
            acc = more if acc is None else acc + more
        if with_slash:
            chosen = [slash_tile(block, place) for place in range(1, nslash)]
            keys = jnp.concatenate([kx[tile_rows(index), :] for index, _ in chosen], axis=0)
            values = jnp.concatenate([vx[tile_rows(index), :] for index, _ in chosen], axis=0)
            scores = dot(keys, query, 1, 1)
            parts = []
            for place, (_, bias) in enumerate(chosen):
                weights = jnp.exp2(
                    scores[place * BLK : (place + 1) * BLK, :] * factor + (bias - base)
                ).astype(BF16)
                sums = sums + sublane_sums(weights.astype(F32))
                parts.append(weights)
            more = dot(values, jnp.concatenate(parts, axis=0), 0, 0)
            acc = more if acc is None else acc + more
        if not first:
            acc = acc_in[rows, :] + acc
        if last:
            return finish(unit, acc, sums, peak)
        out_a[rows, :] = acc
        out_b[stat : stat + 8, :] = sums
        out_b[stat + 8 : stat + 16, :] = peak
        return None

    def redo(unit):
        block = block_from + unit
        query = query_rows(unit)
        copies = []
        row0 = 0
        for place, (kv, mark) in enumerate(spare_refs):
            part = pl.ds(row0, kv.shape[0])
            copies.append(pltpu.make_async_copy(kv, redo_k.at[part, :], redo_sems.at[2 * place]))
            copies.append(
                pltpu.make_async_copy(mark, redo_e.at[part, :], redo_sems.at[2 * place + 1])
            )
            row0 += kv.shape[0]
        for copy in copies:
            copy.start()
        for copy in copies:
            copy.wait()
        if cfg["packs"]:
            redo_k[row0 : row0 + pack_ref.shape[0], :] = pack_ref[...]
            redo_e[row0 : row0 + pack_ref.shape[0], :] = vert_refs[0][1][...]
        redo_acc[...] = jnp.zeros_like(redo_acc)
        redo_stat[0:8, :] = jnp.zeros((8, width), F32)
        redo_stat[8:16, :] = jnp.full((8, width), NEG, F32)

        def merge(scores, values):
            peak = redo_stat[8:16, :]
            high = jnp.maximum(peak, jnp.max(scores, axis=0, keepdims=True))
            weights = jnp.where(scores > 1e-3 * NEG, jnp.exp2(scores - high[:1]), 0.0).astype(BF16)
            shrink = jnp.exp2(peak - high)
            redo_stat[0:8, :] = redo_stat[0:8, :] * shrink + sublane_sums(weights.astype(F32))
            redo_stat[8:16, :] = high
            redo_acc[...] = redo_acc[...] * shrink[:1] + dot(values, weights, 0, 0)

        def slash_step(place, carry):
            index, bias = slash_tile(block, place)
            scores = dot(kx[tile_rows(index), :], query, 1, 1) * factor + bias
            key_at = lax.broadcasted_iota(jnp.int32, scores.shape, 0)
            query_at = lax.broadcasted_iota(jnp.int32, scores.shape, 1) % BLK
            reach = jnp.where(offsets[head_index, place] > 0, BLK, 0)
            merge(jnp.where(key_at <= query_at + reach, scores, NEG), vx[tile_rows(index), :])
            return carry

        def vert_step(tile, carry):
            here = tile_rows(tile)
            keys = jnp.concatenate([redo_k[here, :LANES], redo_e[here, :]], axis=1)
            merge(dot(keys, marked(query, block), 1, 1) * factor, redo_k[here, LANES:])
            return carry

        lax.fori_loop(0, nslash, slash_step, 0)
        lax.fori_loop(0, redo_k.shape[0] // BLK, vert_step, 0)
        finish(unit, redo_acc[...], redo_stat[0:8, :], redo_stat[8:16, :])

    def whole_step(tiles, with_slash, state):
        totals = [one_unit(unit, tiles, with_slash, state) for unit in range(per_step)]
        if last:
            worst = jnp.zeros((1, width), F32)
            for total in totals:
                worst = jnp.maximum(worst, jnp.where(total < LIMIT, 0.0, 1.0))

            @pl.when(jnp.max(worst) > 0.0)
            def _():
                for unit in range(per_step):
                    redo(unit)

    def sized_step(with_slash, state):
        groups = cfg["groups"]
        limited = [g for g, n in enumerate(groups) if n > 2 and cfg["counted"][g] is not None]
        if not limited:
            whole_step(groups, with_slash, state)
            return
        fits = functools.reduce(
            jnp.logical_and, [counts[cfg["counted"][g]] <= 2 * BLK for g in limited]
        )

        @pl.when(fits)
        def _():
            few = [2 if g in limited else n for g, n in enumerate(groups)]
            whole_step(few, with_slash, state)

        @pl.when(jnp.logical_not(fits))
        def _():
            whole_step(groups, with_slash, state)

    slash_from, slash_to = cfg["slash_steps"]
    if slash_from >= slash_to:
        sized_step(False, 0)
    elif slash_from <= 0 and slash_to >= cfg["steps"]:
        sized_step(True, 0)
    else:
        within = (step >= slash_from) & (step < slash_to)

        @pl.when(within)
        def _():
            sized_step(True, 0)

        @pl.when(jnp.logical_not(within))
        def _():
            sized_step(False, cfg["states"] - 1)


def stage(
    offsets, counts, queries, states, verts, counted, sources, spare, *,
    blocks, first=False, last=False, slash=(0, 0), own_tile=0, tiles=0, pack_row0=None,
    per_step=4, cost=6,
):
    rows, columns = queries.shape
    heads = columns // LANES
    width = heads * BLK
    step_from = blocks[0] // per_step
    steps = (blocks[1] - blocks[0]) // per_step
    packs = pack_row0 is not None
    cfg = dict(
        per_step=per_step,
        nblocks=rows // BLK,
        tok_rows=rows,
        step_from=step_from,
        steps=steps,
        slash_steps=((slash[0] - blocks[0]) // per_step, (slash[1] - blocks[0]) // per_step),
        factor=1.0 / (math.sqrt(LANES) * LN2),
        first=first,
        last=last,
        states=len(states),
        own_tile=own_tile,
        groups=[mark.shape[0] // BLK for _, mark in verts],
        counted=counted,
        sources=[(row0, mine.shape[0], fixed) for row0, fixed, mine, _ in sources],
        spares=len(spare),
        packs=packs,
        pack_row0=pack_row0,
    )

    def moving(block_rows, from_step=0, count=steps):
        return pl.BlockSpec(
            (block_rows * per_step, width),
            lambda step, *_: (jnp.clip(step - from_step, 0, count - 1), 0),
        )

    def whole(array):
        return pl.BlockSpec(array.shape, lambda step, *_: (0, 0))

    anywhere = pl.BlockSpec(memory_space=pl.ANY)
    operands = [queries]
    specs = [pl.BlockSpec((BLK * per_step, columns), lambda s, *_: (s + step_from, 0))]
    for (array_a, array_b), from_block in states:
        count = array_a.shape[0] // (BLK * per_step)
        operands += [array_a, array_b]
        from_step = from_block // per_step - step_from
        specs += [moving(BLK, from_step, count), moving(16, from_step, count)]
    for pair in verts:
        operands += list(pair)
        specs += [whole(array) for array in pair]
    for _, _, mine, other in sources:
        operands += [mine, other]
        specs += [anywhere, anywhere]
    for pair in spare:
        operands += list(pair)
        specs += [anywhere, anywhere]
    scratch = []
    if sources:
        scratch += [
            pltpu.VMEM((tiles * BLK, LANES), BF16),
            pltpu.VMEM((tiles * BLK, LANES), BF16),
            pltpu.SemaphoreType.DMA((2 * len(sources),)),
        ]
    slot_pad = verts[0][1].shape[0] if verts else 0
    if packs:
        scratch += [pltpu.VMEM((slot_pad, 2 * LANES), BF16)]
    if last:
        out_shape = [
            jax.ShapeDtypeStruct((rows, columns), BF16),
            jax.ShapeDtypeStruct((heads, rows), F32),
        ]
        out_specs = [
            pl.BlockSpec((BLK * per_step, columns), lambda s, *_: (s, 0)),
            pl.BlockSpec((heads, BLK * per_step), lambda s, *_: (0, s)),
        ]
        spare_rows = sum(kv.shape[0] for kv, _ in spare) + slot_pad * packs
        scratch += [
            pltpu.VMEM((spare_rows, 2 * LANES), BF16),
            pltpu.VMEM((spare_rows, LANES), BF16),
            pltpu.VMEM((BLK, width), F32),
            pltpu.VMEM((16, width), F32),
            pltpu.SemaphoreType.DMA((2 * len(spare),)),
        ]
    else:
        out_shape = [
            jax.ShapeDtypeStruct((steps * per_step * BLK, width), F32),
            jax.ShapeDtypeStruct((steps * per_step * 16, width), F32),
        ]
        out_specs = [moving(BLK), moving(16)]
        if packs:
            out_shape.append(jax.ShapeDtypeStruct((slot_pad, 2 * LANES), BF16))
            out_specs.append(pl.BlockSpec((slot_pad, 2 * LANES), lambda s, *_: (0, 0)))
    return pl.pallas_call(
        functools.partial(stage_kernel, cfg),
        grid_spec=pltpu.PrefetchScalarGridSpec(
            num_scalar_prefetch=2,
            grid=(steps,),
            in_specs=specs,
            out_specs=out_specs,
            scratch_shapes=scratch,
        ),
        out_shape=out_shape,
        compiler_params=pltpu.CompilerParams(vmem_limit_bytes=VMEM_BYTES),
        cost_estimate=pl.CostEstimate(
            flops=cost * 1000000000, bytes_accessed=1 << 20, transcendentals=0
        ),
        name="attend_stage",
    )(offsets, counts, *operands)


def body(queries, key_rows, value_rows, vertical_columns, slash_offsets):
    seq_count = lax.axis_size("seq")
    core = lax.axis_index("rep")
    tok_rows = queries.shape[0]
    nblocks = tok_rows // BLK
    radius = (SPAN + nblocks - 2) // nblocks
    slot_count = 3 * vertical_columns.shape[1] // (2 * seq_count)
    slot_pad = -(-slot_count // BLK) * BLK
    near = radius + 1

    payload = jnp.where(core == 0, key_rows, value_rows)
    everything = (0, nblocks)
    moved = shifted(payload, "seq", 1)

    prepared = prep(
        slash_offsets, vertical_columns, key_rows, value_rows, seq_count, near, slot_pad
    )
    marks, places = prepared[: near + 1], prepared[near + 1 : -2]
    own_pack, counts = prepared[-2:]
    run = functools.partial(stage, slash_offsets, counts, queries, blocks=everything)

    own_verts = (own_pack, marks[0])
    own_row0 = radius * tok_rows
    far_moved = []
    if seq_count > near:
        far_payload = jnp.where(core == 0, own_pack[:, :LANES], own_pack[:, LANES:])
        far_moved = [
            shifted(far_payload, "seq", distance) for distance in range(near, seq_count)
        ]
    state = run(
        [], [own_verts], [0], [(0, True, key_rows, value_rows)], [], first=True, tiles=nblocks
    )
    moved, state, far_moved = after(moved, state, far_moved)
    moved2 = shifted(moved, "seq", 1)
    hop1 = (moved, swapped(moved))

    far_verts = []
    if far_moved:
        rows = []
        for mine in far_moved:
            other = swapped(mine)
            rows.append(
                jnp.where(
                    core == 0,
                    jnp.concatenate([mine, other], axis=1),
                    jnp.concatenate([other, mine], axis=1),
                )
            )
        far_verts = [(jnp.concatenate(rows, axis=0) if len(rows) > 1 else rows[0], marks[near])]

    *state, hop_pack = run(
        [(state, 0)], [(places[1], marks[1])] + far_verts, [1] + [None] * len(far_verts),
        [(0, False) + hop1], [], tiles=nblocks, pack_row0=0,
    )
    moved2, state = after(moved2, state)
    return tuple(
        run(
            [(state, 0)], [(places[2], marks[2])], [2],
            [
                (0, False, moved2, swapped(moved2)),
                (own_row0 - tok_rows, False) + hop1,
                (own_row0, True, key_rows, value_rows),
            ],
            [own_verts, (hop_pack, marks[1])] + far_verts,
            last=True, slash=everything, own_tile=radius * nblocks,
            tiles=(radius + 1) * nblocks, pack_row0=0,
        )
    )


def solution(mesh):
    placed = (
        P(("groups", "seq"), ("head", "rep")),
        P(("groups", "seq"), "head"),
        P(("groups", "seq"), "head"),
        P("groups", None),
        P("groups", None),
    )
    return jax.shard_map(
        body,
        mesh=mesh,
        in_specs=placed,
        out_specs=(P(("groups", "seq"), ("head", "rep")), P(("head", "rep"), ("groups", "seq"))),
        check_vma=False,
    )
```

```python
import functools
import math

import jax
import jax.numpy as jnp
from jax import lax
from jax.experimental import pallas as pl
from jax.experimental.pallas import tpu as pltpu
from jax.sharding import PartitionSpec as P

BLK = 128
SPAN = 32
LANES = 128
NEG = -1e30
LIMIT = 1e30
EARLY = (2, 3)
LN2 = math.log(2.0)
VMEM_BYTES = 30 * 1024 * 1024
BF16 = jnp.bfloat16
F32 = jnp.float32


def shifted(value, axis, steps):
    count = lax.axis_size(axis)
    leading, last = (max(0, -steps), min(count, count - steps))
    return lax.ppermute(value, axis, [(source, source + steps) for source in range(leading, last)])


def swapped(value):
    return lax.ppermute(value, "rep", [(0, 1), (1, 0)])


def after(*values):
    return lax.optimization_barrier(values)


def dot(left, right, left_dim, right_dim):
    return lax.dot_general(
        left, right, (((left_dim,), (right_dim,)), ((), ())), preferred_element_type=F32
    )


def sublane_sums(values):
    return jnp.sum(values.reshape(-1, 8, values.shape[1]), axis=0)


def one_hot_rows(places, rows_of, count):
    total = jnp.zeros((places.shape[0], 2 * LANES), F32)
    for start in range(0, count, 512):
        hot = jnp.concatenate(
            [
                jnp.where(
                    places
                    == lax.broadcasted_iota(jnp.int32, places.shape, 1) + (start + lane0),
                    1.0,
                    0.0,
                ).astype(BF16)
                for lane0 in range(0, 512, LANES)
            ],
            axis=1,
        )
        total = total + dot(hot, rows_of(start, 512), 1, 0)
    return total.astype(BF16)


def prep_kernel(cfg, offsets, columns_hbm, k_hbm, v_hbm, *refs):
    *refs, columns_ref, k_ref, v_ref, sems = refs
    moves = [
        pltpu.make_async_copy(source, target, sems.at[place])
        for place, (source, target) in enumerate(
            ((columns_hbm, columns_ref), (k_hbm, k_ref), (v_hbm, v_ref))
        )
    ]
    for move in moves:
        move.start()
    tok_rows, slot_pad, near = cfg["tok_rows"], cfg["slot_pad"], cfg["near"]
    marks, places, packed, counts = refs[: near + 1], refs[near + 1 : -2], refs[-2], refs[-1]
    seq_index = lax.axis_index("seq")
    head_index = lax.axis_index("head")
    nvert = columns_ref.shape[1]
    nblocks = tok_rows // BLK
    moves[0].wait()
    columns = columns_ref[pl.ds(head_index, 1), :]
    wide = jnp.broadcast_to(columns, (8, nvert))
    shifts = [offsets[head_index, place] // BLK for place in range(offsets.shape[1])]

    def ahead_of(start):
        return jnp.sum((columns < start).astype(jnp.int32))

    after = ahead_of((seq_index + 1) * tok_rows)
    for distance in range(cfg["seq_count"]):
        start = (seq_index - distance) * tok_rows
        ahead = ahead_of(start)
        turned = pltpu.roll(wide, lax.rem(nvert - ahead, nvert), 1)
        if distance < near:
            counts[distance] = after - ahead
        after = ahead
        for tile in range(slot_pad // BLK):
            part = slice(tile * BLK, (tile + 1) * BLK)
            listed = jnp.broadcast_to(turned[0:1, part], (BLK, BLK)).T
            inside = (listed >= start) & (listed < start + tok_rows) & (start >= 0)
            lane = lax.broadcasted_iota(jnp.int32, listed.shape, 1)
            gap = seq_index * nblocks + lane - lax.shift_right_arithmetic(listed, 7)
            seen = inside & (gap > 0)
            for shift in shifts:
                seen = seen & (gap != shift)
            where = slice(tile * BLK, (tile + 1) * BLK)
            if distance >= near:
                row0 = (distance - near) * slot_pad + tile * BLK
                where = slice(row0, row0 + BLK)
            marks[min(distance, near)][where, :] = jnp.where(seen, 0.0, NEG).astype(BF16)
            if distance < near:
                places[distance][where, :] = jnp.where(inside, listed - start, -1)
    moves[1].wait()
    moves[2].wait()
    packed[...] = one_hot_rows(
        places[0][...],
        lambda row0, rows: jnp.concatenate(
            [k_ref[row0 : row0 + rows, :], v_ref[row0 : row0 + rows, :]], axis=1
        ),
        tok_rows,
    )


def prep(offsets, columns, key_rows, value_rows, seq_count, near, slot_pad):
    def whole(shape):
        return pl.BlockSpec(shape, lambda step, offsets: (0, 0))

    far_rows = max(seq_count - near, 1) * slot_pad
    shapes = [(slot_pad, LANES)] * near + [(far_rows, LANES)]
    places = [(slot_pad, LANES)] * near
    return pl.pallas_call(
        functools.partial(
            prep_kernel,
            dict(tok_rows=key_rows.shape[0], slot_pad=slot_pad, near=near, seq_count=seq_count),
        ),
        grid_spec=pltpu.PrefetchScalarGridSpec(
            num_scalar_prefetch=1,
            grid=(1,),
            in_specs=[pl.BlockSpec(memory_space=pltpu.HBM)] * 3,
            out_specs=[whole(shape) for shape in shapes + places + [(slot_pad, 2 * LANES)]]
            + [pl.BlockSpec(memory_space=pltpu.SMEM)],
            scratch_shapes=[
                pltpu.VMEM(columns.shape, jnp.int32),
                pltpu.VMEM(key_rows.shape, BF16),
                pltpu.VMEM(value_rows.shape, BF16),
                pltpu.SemaphoreType.DMA((3,)),
            ],
        ),
        out_shape=[jax.ShapeDtypeStruct(shape, BF16) for shape in shapes]
        + [jax.ShapeDtypeStruct(shape, jnp.int32) for shape in places]
        + [
            jax.ShapeDtypeStruct((slot_pad, 2 * LANES), BF16),
            jax.ShapeDtypeStruct((8,), jnp.int32),
        ],
        compiler_params=pltpu.CompilerParams(vmem_limit_bytes=VMEM_BYTES),
        cost_estimate=pl.CostEstimate(flops=1 << 31, bytes_accessed=1 << 20, transcendentals=0),
        name="prepare",
    )(offsets, columns, key_rows, value_rows)


def stage_kernel(cfg, offsets, counts, q_ref, *refs):
    refs = list(refs)
    nslash = offsets.shape[1]
    heads = q_ref.shape[1] // LANES
    width = heads * BLK
    per_step = cfg["per_step"]
    factor = cfg["factor"]
    first, last = cfg["first"], cfg["last"]
    sources = cfg["sources"]
    step = pl.program_id(0)
    block_from = cfg["step_from"] * per_step + step * per_step
    block0 = lax.axis_index("seq") * cfg["nblocks"]
    core = lax.axis_index("rep")
    head_index = lax.axis_index("head")

    state_refs = [(refs.pop(0), refs.pop(0)) for _ in range(cfg["states"])]
    vert_refs = [[refs.pop(0), refs.pop(0)] for _ in cfg["groups"]]
    source_refs = [(refs.pop(0), refs.pop(0)) for _ in sources]
    spare_refs = [(refs.pop(0), refs.pop(0)) for _ in range(cfg["spares"])]
    out_a, out_b = refs.pop(0), refs.pop(0)
    pack_out = refs.pop(0) if cfg["packs"] and not last else None
    if sources:
        kx, vx, sems = refs.pop(0), refs.pop(0), refs.pop(0)
    if cfg["packs"]:
        pack_ref = refs.pop(0)
    if last:
        redo_k, redo_e, redo_acc, redo_stat, redo_sems, redo_flag = refs

    def source_copies(swap):
        copies = []
        for place, ((row0, rows, fixed), (mine, other)) in enumerate(zip(sources, source_refs)):
            targets = (vx, kx) if swap and not fixed else (kx, vx)
            for which, (ref, target) in enumerate(zip((mine, other), targets)):
                copies.append(
                    pltpu.make_async_copy(
                        ref, target.at[pl.ds(row0, rows), :], sems.at[2 * place + which]
                    )
                )
        return copies

    if sources:

        @pl.when(step == 0)
        def _():
            @pl.when(core == 0)
            def _():
                for copy in source_copies(False):
                    copy.start()

            @pl.when(core != 0)
            def _():
                for copy in source_copies(True):
                    copy.start()

            waits = source_copies(False)
            for copy in waits[:2]:
                copy.wait()
            if cfg["packs"]:
                row0 = cfg["pack_row0"]
                pack_ref[...] = one_hot_rows(
                    vert_refs[0][0][...],
                    lambda at, rows: jnp.concatenate(
                        [
                            kx[row0 + at : row0 + at + rows, :],
                            vx[row0 + at : row0 + at + rows, :],
                        ],
                        axis=1,
                    ),
                    cfg["tok_rows"],
                )
                if pack_out is not None:
                    pack_out[...] = pack_ref[...]
            for copy in waits[2:]:
                copy.wait()

    if cfg["packs"]:
        vert_refs[0][0] = pack_ref

    def tile_rows(index):
        return pl.ds(pl.multiple_of(index * BLK, BLK), BLK)

    def slash_tile(block, place):
        shift = offsets[head_index, place] // BLK
        bias = jnp.where(block0 + block - shift >= 0, 0.0, NEG).astype(F32)
        return jnp.maximum(cfg["own_tile"] + block - shift, 0), bias

    def span(unit):
        start = unit * BLK
        return pl.ds(start if isinstance(unit, int) else pl.multiple_of(start, BLK), BLK)

    def query_rows(unit):
        rows = span(unit)
        return jnp.concatenate(
            [q_ref[rows, h * LANES : (h + 1) * LANES] for h in range(heads)], axis=0
        )

    def marked(query, block):
        lane = lax.broadcasted_iota(jnp.int32, (query.shape[0], LANES), 1)
        return jnp.concatenate([query, jnp.where(lane == block, 1.0, 0.0).astype(BF16)], axis=1)

    def finish(unit, acc, sums, peak):
        total = jnp.sum(sums, axis=0, keepdims=True)
        result = (acc * (1.0 / total)).astype(BF16)
        norm = peak[:1] * LN2 + jnp.log(total)
        for h in range(heads):
            part = slice(h * LANES, (h + 1) * LANES)
            out_a[span(unit), part] = result[:, part].T
            out_b[h : h + 1, span(unit)] = norm[:, part]
        return total

    def one_unit(unit, tiles, chosen_places):
        block = block_from + unit
        query = query_rows(unit)
        rows = slice(unit * BLK, (unit + 1) * BLK)
        stat = 2 * 8 * unit
        acc = sums = None
        if first:
            own = tile_rows(cfg["own_tile"] + block)
            scores = dot(kx[own, :], query, 1, 1)
            key_at = lax.broadcasted_iota(jnp.int32, scores.shape, 0)
            query_at = lax.broadcasted_iota(jnp.int32, scores.shape, 1) % BLK
            scores = jnp.where(key_at <= query_at, scores, NEG) * factor
            peak = jnp.broadcast_to(jnp.max(scores, axis=0, keepdims=True), (8, width))
            weights = jnp.exp2(scores - peak[:1]).astype(BF16)
            sums = sublane_sums(weights.astype(F32))
            acc = dot(vx[own, :], weights, 0, 0)
        else:
            acc_in, stat_in = state_refs[0]
            sums = stat_in[stat : stat + 8, :]
            peak = stat_in[stat + 8 : stat + 16, :]
        base = peak[:1]
        if sum(tiles):
            keys = jnp.concatenate(
                [
                    jnp.concatenate([kv[: n * BLK, :LANES], mark[: n * BLK, :]], axis=1)
                    for n, (kv, mark) in zip(tiles, vert_refs)
                    if n
                ],
                axis=0,
            )
            values = jnp.concatenate(
                [kv[: n * BLK, LANES:] for n, (kv, _) in zip(tiles, vert_refs) if n], axis=0
            )
            weights = jnp.exp2(dot(keys, marked(query, block), 1, 1) * factor - base).astype(BF16)
            sums = sums + sublane_sums(weights.astype(F32))
            more = dot(values, weights, 0, 0)
            acc = more if acc is None else acc + more
        if chosen_places:
            chosen = [slash_tile(block, place) for place in chosen_places]
            keys = jnp.concatenate([kx[tile_rows(index), :] for index, _ in chosen], axis=0)
            values = jnp.concatenate([vx[tile_rows(index), :] for index, _ in chosen], axis=0)
            scores = dot(keys, query, 1, 1)
            parts = []
            for place, (_, bias) in enumerate(chosen):
                weights = jnp.exp2(
                    scores[place * BLK : (place + 1) * BLK, :] * factor + (bias - base)
                ).astype(BF16)
                sums = sums + sublane_sums(weights.astype(F32))
                parts.append(weights)
            more = dot(values, jnp.concatenate(parts, axis=0), 0, 0)
            acc = more if acc is None else acc + more
        if not first:
            acc = acc_in[rows, :] + acc
        if last:
            return finish(unit, acc, sums, peak)
        out_a[rows, :] = acc
        out_b[stat : stat + 8, :] = sums
        out_b[stat + 8 : stat + 16, :] = peak
        return None

    def redo(unit):
        block = block_from + unit
        query = query_rows(unit)
        copies = []
        row0 = 0
        for place, (kv, mark) in enumerate(spare_refs):
            part = pl.ds(row0, kv.shape[0])
            copies.append(pltpu.make_async_copy(kv, redo_k.at[part, :], redo_sems.at[2 * place]))
            copies.append(
                pltpu.make_async_copy(mark, redo_e.at[part, :], redo_sems.at[2 * place + 1])
            )
            row0 += kv.shape[0]
        for copy in copies:
            copy.start()
        for copy in copies:
            copy.wait()
        if cfg["packs"]:
            redo_k[row0 : row0 + pack_ref.shape[0], :] = pack_ref[...]
            redo_e[row0 : row0 + pack_ref.shape[0], :] = vert_refs[0][1][...]
        redo_acc[...] = jnp.zeros_like(redo_acc)
        redo_stat[0:8, :] = jnp.zeros((8, width), F32)
        redo_stat[8:16, :] = jnp.full((8, width), NEG, F32)

        def merge(scores, values):
            peak = redo_stat[8:16, :]
            high = jnp.maximum(peak, jnp.max(scores, axis=0, keepdims=True))
            weights = jnp.where(scores > 1e-3 * NEG, jnp.exp2(scores - high[:1]), 0.0).astype(BF16)
            shrink = jnp.exp2(peak - high)
            redo_stat[0:8, :] = redo_stat[0:8, :] * shrink + sublane_sums(weights.astype(F32))
            redo_stat[8:16, :] = high
            redo_acc[...] = redo_acc[...] * shrink[:1] + dot(values, weights, 0, 0)

        def slash_step(place, carry):
            index, bias = slash_tile(block, place)
            scores = dot(kx[tile_rows(index), :], query, 1, 1) * factor + bias
            key_at = lax.broadcasted_iota(jnp.int32, scores.shape, 0)
            query_at = lax.broadcasted_iota(jnp.int32, scores.shape, 1) % BLK
            reach = jnp.where(offsets[head_index, place] > 0, BLK, 0)
            merge(jnp.where(key_at <= query_at + reach, scores, NEG), vx[tile_rows(index), :])
            return carry

        def vert_step(tile, carry):
            here = tile_rows(tile)
            keys = jnp.concatenate([redo_k[here, :LANES], redo_e[here, :]], axis=1)
            merge(dot(keys, marked(query, block), 1, 1) * factor, redo_k[here, LANES:])
            return carry

        lax.fori_loop(0, nslash, slash_step, 0)
        lax.fori_loop(0, redo_k.shape[0] // BLK, vert_step, 0)
        finish(unit, redo_acc[...], redo_stat[0:8, :], redo_stat[8:16, :])

    def redo_one(unit, carry):
        redo(unit)
        return carry

    def whole_step(tiles, chosen_places):
        totals = [one_unit(unit, tiles, chosen_places) for unit in range(per_step)]
        if last:
            worst = jnp.zeros((1, width), F32)
            for total in totals:
                worst = jnp.maximum(worst, jnp.where(total < LIMIT, 0.0, 1.0))
            redo_flag[0] = jnp.where(jnp.max(worst) > 0.0, 1, 0)

    groups = cfg["groups"]
    limited = [g for g, n in enumerate(groups) if n > 2 and cfg["counted"][g] is not None]
    few = [2 if g in limited else n for g, n in enumerate(groups)]
    fits = functools.reduce(
        jnp.logical_and, [counts[cfg["counted"][g]] <= 2 * BLK for g in limited], step >= 0
    )
    every = list(range(1, nslash))

    def sized_step(wanted, places):
        if limited:

            @pl.when(jnp.logical_and(fits, wanted))
            def _():
                whole_step(few, places)

        @pl.when(jnp.logical_and(jnp.logical_not(fits), wanted) if limited else wanted)
        def _():
            whole_step(groups, places)

    if not cfg["ahead"]:
        sized_step(step >= 0, [])
        return
    share = cfg["steps"] // len(cfg["ahead"])
    for part, ahead in enumerate(cfg["ahead"]):
        within = (step >= part * share) & (step < (part + 1) * share)
        early = offsets[head_index, ahead] <= cfg["tok_rows"] + part * share * per_step * BLK
        sized_step(jnp.logical_and(within, early), every[ahead:] if last else every[:ahead])

        @pl.when(jnp.logical_and(within, jnp.logical_not(early)))
        def _():
            whole_step(groups, every if last else [])

    if last:

        @pl.when(redo_flag[0] > 0)
        def _():
            lax.fori_loop(0, per_step, redo_one, 0)


def stage(
    offsets, counts, queries, states, verts, counted, sources, spare, *,
    blocks, first=False, last=False, ahead=(), own_tile=0, tiles=0, pack_row0=None,
    per_step=4, cost=6,
):
    rows, columns = queries.shape
    heads = columns // LANES
    width = heads * BLK
    step_from = blocks[0] // per_step
    steps = (blocks[1] - blocks[0]) // per_step
    packs = pack_row0 is not None
    cfg = dict(
        per_step=per_step,
        nblocks=rows // BLK,
        tok_rows=rows,
        step_from=step_from,
        steps=steps,
        ahead=ahead,
        factor=1.0 / (math.sqrt(LANES) * LN2),
        first=first,
        last=last,
        states=len(states),
        own_tile=own_tile,
        groups=[mark.shape[0] // BLK for _, mark in verts],
        counted=counted,
        sources=[(row0, mine.shape[0], fixed) for row0, fixed, mine, _ in sources],
        spares=len(spare),
        packs=packs,
        pack_row0=pack_row0,
    )

    def moving(block_rows, from_step=0, count=steps):
        return pl.BlockSpec(
            (block_rows * per_step, width),
            lambda step, *_: (jnp.clip(step - from_step, 0, count - 1), 0),
        )

    def whole(array):
        return pl.BlockSpec(array.shape, lambda step, *_: (0, 0))

    anywhere = pl.BlockSpec(memory_space=pl.ANY)
    operands = [queries]
    specs = [pl.BlockSpec((BLK * per_step, columns), lambda s, *_: (s + step_from, 0))]
    for (array_a, array_b), from_block in states:
        count = array_a.shape[0] // (BLK * per_step)
        operands += [array_a, array_b]
        from_step = from_block // per_step - step_from
        specs += [moving(BLK, from_step, count), moving(16, from_step, count)]
    for pair in verts:
        operands += list(pair)
        specs += [whole(array) for array in pair]
    for _, _, mine, other in sources:
        operands += [mine, other]
        specs += [anywhere, anywhere]
    for pair in spare:
        operands += list(pair)
        specs += [anywhere, anywhere]
    scratch = []
    if sources:
        scratch += [
            pltpu.VMEM((tiles * BLK, LANES), BF16),
            pltpu.VMEM((tiles * BLK, LANES), BF16),
            pltpu.SemaphoreType.DMA((2 * len(sources),)),
        ]
    slot_pad = verts[0][1].shape[0] if verts else 0
    if packs:
        scratch += [pltpu.VMEM((slot_pad, 2 * LANES), BF16)]
    if last:
        out_shape = [
            jax.ShapeDtypeStruct((rows, columns), BF16),
            jax.ShapeDtypeStruct((heads, rows), F32),
        ]
        out_specs = [
            pl.BlockSpec((BLK * per_step, columns), lambda s, *_: (s, 0)),
            pl.BlockSpec((heads, BLK * per_step), lambda s, *_: (0, s)),
        ]
        spare_rows = sum(kv.shape[0] for kv, _ in spare) + slot_pad * packs
        scratch += [
            pltpu.VMEM((spare_rows, 2 * LANES), BF16),
            pltpu.VMEM((spare_rows, LANES), BF16),
            pltpu.VMEM((BLK, width), F32),
            pltpu.VMEM((16, width), F32),
            pltpu.SemaphoreType.DMA((2 * len(spare),)),
            pltpu.SMEM((1,), jnp.int32),
        ]
    else:
        out_shape = [
            jax.ShapeDtypeStruct((steps * per_step * BLK, width), F32),
            jax.ShapeDtypeStruct((steps * per_step * 16, width), F32),
        ]
        out_specs = [moving(BLK), moving(16)]
        if packs:
            out_shape.append(jax.ShapeDtypeStruct((slot_pad, 2 * LANES), BF16))
            out_specs.append(pl.BlockSpec((slot_pad, 2 * LANES), lambda s, *_: (0, 0)))
    return pl.pallas_call(
        functools.partial(stage_kernel, cfg),
        grid_spec=pltpu.PrefetchScalarGridSpec(
            num_scalar_prefetch=2,
            grid=(steps,),
            in_specs=specs,
            out_specs=out_specs,
            scratch_shapes=scratch,
        ),
        out_shape=out_shape,
        compiler_params=pltpu.CompilerParams(vmem_limit_bytes=VMEM_BYTES),
        cost_estimate=pl.CostEstimate(
            flops=cost * 1000000000, bytes_accessed=1 << 20, transcendentals=0
        ),
        name="attend_stage",
    )(offsets, counts, *operands)


def body(queries, key_rows, value_rows, vertical_columns, slash_offsets):
    seq_count = lax.axis_size("seq")
    core = lax.axis_index("rep")
    tok_rows = queries.shape[0]
    nblocks = tok_rows // BLK
    radius = (SPAN + nblocks - 2) // nblocks
    slot_count = 3 * vertical_columns.shape[1] // (2 * seq_count)
    slot_pad = -(-slot_count // BLK) * BLK
    near = radius + 1

    payload = jnp.where(core == 0, key_rows, value_rows)
    everything = (0, nblocks)
    moved = shifted(payload, "seq", 1)

    prepared = prep(
        slash_offsets, vertical_columns, key_rows, value_rows, seq_count, near, slot_pad
    )
    marks, places = prepared[: near + 1], prepared[near + 1 : -2]
    own_pack, counts = prepared[-2:]
    run = functools.partial(stage, slash_offsets, counts, queries, blocks=everything)

    own_verts = (own_pack, marks[0])
    own_row0 = radius * tok_rows
    far_moved = []
    if seq_count > near:
        far_payload = jnp.where(core == 0, own_pack[:, :LANES], own_pack[:, LANES:])
        far_moved = [
            shifted(far_payload, "seq", distance) for distance in range(near, seq_count)
        ]
    state = run(
        [], [own_verts], [0], [(0, True, key_rows, value_rows)], [], first=True, tiles=nblocks
    )
    moved, state, far_moved = after(moved, state, far_moved)
    moved2 = shifted(moved, "seq", 1)
    hop1 = (moved, swapped(moved))

    far_verts = []
    if far_moved:
        rows = []
        for mine in far_moved:
            other = swapped(mine)
            rows.append(
                jnp.where(
                    core == 0,
                    jnp.concatenate([mine, other], axis=1),
                    jnp.concatenate([other, mine], axis=1),
                )
            )
        far_verts = [(jnp.concatenate(rows, axis=0) if len(rows) > 1 else rows[0], marks[near])]

    *state, hop_pack = run(
        [(state, 0)], [(places[1], marks[1])] + far_verts, [1] + [None] * len(far_verts),
        [(0, False) + hop1, (tok_rows, True, key_rows, value_rows)], [], ahead=EARLY,
        own_tile=nblocks, tiles=2 * nblocks, pack_row0=0,
    )
    moved2, state = after(moved2, state)
    return tuple(
        run(
            [(state, 0)], [(places[2], marks[2])], [2],
            [
                (0, False, moved2, swapped(moved2)),
                (own_row0 - tok_rows, False) + hop1,
                (own_row0, True, key_rows, value_rows),
            ],
            [own_verts, (hop_pack, marks[1])] + far_verts,
            last=True, ahead=EARLY, own_tile=radius * nblocks,
            tiles=(radius + 1) * nblocks, pack_row0=0,
        )
    )


def solution(mesh):
    placed = (
        P(("groups", "seq"), ("head", "rep")),
        P(("groups", "seq"), "head"),
        P(("groups", "seq"), "head"),
        P("groups", None),
        P("groups", None),
    )
    return jax.shard_map(
        body,
        mesh=mesh,
        in_specs=placed,
        out_specs=(P(("groups", "seq"), ("head", "rep")), P(("head", "rep"), ("groups", "seq"))),
        check_vma=False,
    )
```

```python
import functools
import math

import jax
import jax.numpy as jnp
from jax import lax
from jax.experimental import pallas as pl
from jax.experimental.pallas import tpu as pltpu
from jax.sharding import PartitionSpec as P

BLK = 128
SPAN = 32
LANES = 128
NEG = -1e30
LIMIT = 1e30
EARLY = (2, 2, 3, 4)
LN2 = math.log(2.0)
VMEM_BYTES = 30 * 1024 * 1024
BF16 = jnp.bfloat16
F32 = jnp.float32


def shifted(value, axis, steps):
    count = lax.axis_size(axis)
    leading, last = (max(0, -steps), min(count, count - steps))
    return lax.ppermute(value, axis, [(source, source + steps) for source in range(leading, last)])


def swapped(value):
    return lax.ppermute(value, "rep", [(0, 1), (1, 0)])


def after(*values):
    return lax.optimization_barrier(values)


def dot(left, right, left_dim, right_dim):
    return lax.dot_general(
        left, right, (((left_dim,), (right_dim,)), ((), ())), preferred_element_type=F32
    )


def sublane_sums(values):
    return jnp.sum(values.reshape(-1, 8, values.shape[1]), axis=0)


def one_hot_rows(places, rows_of, count):
    total = jnp.zeros((places.shape[0], 2 * LANES), F32)
    for start in range(0, count, 512):
        hot = jnp.concatenate(
            [
                jnp.where(
                    places
                    == lax.broadcasted_iota(jnp.int32, places.shape, 1) + (start + lane0),
                    1.0,
                    0.0,
                ).astype(BF16)
                for lane0 in range(0, 512, LANES)
            ],
            axis=1,
        )
        total = total + dot(hot, rows_of(start, 512), 1, 0)
    return total.astype(BF16)


def prep_kernel(cfg, offsets, columns_hbm, k_hbm, v_hbm, *refs):
    *refs, columns_ref, k_ref, v_ref, sems = refs
    moves = [
        pltpu.make_async_copy(source, target, sems.at[place])
        for place, (source, target) in enumerate(
            ((columns_hbm, columns_ref), (k_hbm, k_ref), (v_hbm, v_ref))
        )
    ]
    for move in moves:
        move.start()
    tok_rows, slot_pad, near = cfg["tok_rows"], cfg["slot_pad"], cfg["near"]
    marks, places, packed, counts = refs[: near + 1], refs[near + 1 : -2], refs[-2], refs[-1]
    seq_index = lax.axis_index("seq")
    head_index = lax.axis_index("head")
    nvert = columns_ref.shape[1]
    nblocks = tok_rows // BLK
    moves[0].wait()
    columns = columns_ref[pl.ds(head_index, 1), :]
    wide = jnp.broadcast_to(columns, (8, nvert))
    shifts = [offsets[head_index, place] // BLK for place in range(offsets.shape[1])]

    def ahead_of(start):
        return jnp.sum((columns < start).astype(jnp.int32))

    after = ahead_of((seq_index + 1) * tok_rows)
    for distance in range(cfg["seq_count"]):
        start = (seq_index - distance) * tok_rows
        ahead = ahead_of(start)
        turned = pltpu.roll(wide, lax.rem(nvert - ahead, nvert), 1)
        if distance < near:
            counts[distance] = after - ahead
        after = ahead
        for tile in range(slot_pad // BLK):
            part = slice(tile * BLK, (tile + 1) * BLK)
            listed = jnp.broadcast_to(turned[0:1, part], (BLK, BLK)).T
            inside = (listed >= start) & (listed < start + tok_rows) & (start >= 0)
            lane = lax.broadcasted_iota(jnp.int32, listed.shape, 1)
            gap = seq_index * nblocks + lane - lax.shift_right_arithmetic(listed, 7)
            seen = inside & (gap > 0)
            for shift in shifts:
                seen = seen & (gap != shift)
            where = slice(tile * BLK, (tile + 1) * BLK)
            if distance >= near:
                row0 = (distance - near) * slot_pad + tile * BLK
                where = slice(row0, row0 + BLK)
            marks[min(distance, near)][where, :] = jnp.where(seen, 0.0, NEG).astype(BF16)
            if distance < near:
                places[distance][where, :] = jnp.where(inside, listed - start, -1)
    moves[1].wait()
    moves[2].wait()
    packed[...] = one_hot_rows(
        places[0][...],
        lambda row0, rows: jnp.concatenate(
            [k_ref[row0 : row0 + rows, :], v_ref[row0 : row0 + rows, :]], axis=1
        ),
        tok_rows,
    )


def prep(offsets, columns, key_rows, value_rows, seq_count, near, slot_pad):
    def whole(shape):
        return pl.BlockSpec(shape, lambda step, offsets: (0, 0))

    far_rows = max(seq_count - near, 1) * slot_pad
    shapes = [(slot_pad, LANES)] * near + [(far_rows, LANES)]
    places = [(slot_pad, LANES)] * near
    return pl.pallas_call(
        functools.partial(
            prep_kernel,
            dict(tok_rows=key_rows.shape[0], slot_pad=slot_pad, near=near, seq_count=seq_count),
        ),
        grid_spec=pltpu.PrefetchScalarGridSpec(
            num_scalar_prefetch=1,
            grid=(1,),
            in_specs=[pl.BlockSpec(memory_space=pltpu.HBM)] * 3,
            out_specs=[whole(shape) for shape in shapes + places + [(slot_pad, 2 * LANES)]]
            + [pl.BlockSpec(memory_space=pltpu.SMEM)],
            scratch_shapes=[
                pltpu.VMEM(columns.shape, jnp.int32),
                pltpu.VMEM(key_rows.shape, BF16),
                pltpu.VMEM(value_rows.shape, BF16),
                pltpu.SemaphoreType.DMA((3,)),
            ],
        ),
        out_shape=[jax.ShapeDtypeStruct(shape, BF16) for shape in shapes]
        + [jax.ShapeDtypeStruct(shape, jnp.int32) for shape in places]
        + [
            jax.ShapeDtypeStruct((slot_pad, 2 * LANES), BF16),
            jax.ShapeDtypeStruct((8,), jnp.int32),
        ],
        compiler_params=pltpu.CompilerParams(vmem_limit_bytes=VMEM_BYTES),
        cost_estimate=pl.CostEstimate(flops=1 << 31, bytes_accessed=1 << 20, transcendentals=0),
        name="prepare",
    )(offsets, columns, key_rows, value_rows)


def stage_kernel(cfg, offsets, counts, q_ref, *refs):
    refs = list(refs)
    nslash = offsets.shape[1]
    heads = q_ref.shape[1] // LANES
    width = heads * BLK
    per_step = cfg["per_step"]
    factor = cfg["factor"]
    first, last = cfg["first"], cfg["last"]
    sources = cfg["sources"]
    step = pl.program_id(0)
    block_from = cfg["step_from"] * per_step + step * per_step
    block0 = lax.axis_index("seq") * cfg["nblocks"]
    core = lax.axis_index("rep")
    head_index = lax.axis_index("head")

    state_refs = [(refs.pop(0), refs.pop(0)) for _ in range(cfg["states"])]
    vert_refs = [[refs.pop(0), refs.pop(0)] for _ in cfg["groups"]]
    source_refs = [(refs.pop(0), refs.pop(0)) for _ in sources]
    spare_refs = [(refs.pop(0), refs.pop(0)) for _ in range(cfg["spares"])]
    out_a, out_b = refs.pop(0), refs.pop(0)
    pack_out = refs.pop(0) if cfg["packs"] and not last else None
    if sources:
        kx, vx, sems = refs.pop(0), refs.pop(0), refs.pop(0)
    if cfg["packs"]:
        pack_ref = refs.pop(0)
    if last:
        redo_k, redo_e, redo_acc, redo_stat, redo_sems, redo_flag = refs

    def source_copies(swap):
        copies = []
        for place, ((row0, rows, fixed), (mine, other)) in enumerate(zip(sources, source_refs)):
            targets = (vx, kx) if swap and not fixed else (kx, vx)
            for which, (ref, target) in enumerate(zip((mine, other), targets)):
                copies.append(
                    pltpu.make_async_copy(
                        ref, target.at[pl.ds(row0, rows), :], sems.at[2 * place + which]
                    )
                )
        return copies

    if sources:

        @pl.when(step == 0)
        def _():
            @pl.when(core == 0)
            def _():
                for copy in source_copies(False):
                    copy.start()

            @pl.when(core != 0)
            def _():
                for copy in source_copies(True):
                    copy.start()

            waits = source_copies(False)
            for copy in waits[:2]:
                copy.wait()
            if cfg["packs"]:
                row0 = cfg["pack_row0"]
                pack_ref[...] = one_hot_rows(
                    vert_refs[0][0][...],
                    lambda at, rows: jnp.concatenate(
                        [
                            kx[row0 + at : row0 + at + rows, :],
                            vx[row0 + at : row0 + at + rows, :],
                        ],
                        axis=1,
                    ),
                    cfg["tok_rows"],
                )
                if pack_out is not None:
                    pack_out[...] = pack_ref[...]
            for copy in waits[2:]:
                copy.wait()

    if cfg["packs"]:
        vert_refs[0][0] = pack_ref

    def tile_rows(index):
        return pl.ds(pl.multiple_of(index * BLK, BLK), BLK)

    def slash_tile(block, place):
        shift = offsets[head_index, place] // BLK
        bias = jnp.where(block0 + block - shift >= 0, 0.0, NEG).astype(F32)
        return jnp.maximum(cfg["own_tile"] + block - shift, 0), bias

    def span(unit):
        start = unit * BLK
        return pl.ds(start if isinstance(unit, int) else pl.multiple_of(start, BLK), BLK)

    def query_rows(unit):
        rows = span(unit)
        return jnp.concatenate(
            [q_ref[rows, h * LANES : (h + 1) * LANES] for h in range(heads)], axis=0
        )

    def marked(query, block):
        lane = lax.broadcasted_iota(jnp.int32, (query.shape[0], LANES), 1)
        return jnp.concatenate([query, jnp.where(lane == block, 1.0, 0.0).astype(BF16)], axis=1)

    def finish(unit, acc, sums, peak):
        total = jnp.sum(sums, axis=0, keepdims=True)
        result = (acc * (1.0 / total)).astype(BF16)
        norm = peak[:1] * LN2 + jnp.log(total)
        for h in range(heads):
            part = slice(h * LANES, (h + 1) * LANES)
            out_a[span(unit), part] = result[:, part].T
            out_b[h : h + 1, span(unit)] = norm[:, part]
        return total

    def one_unit(unit, tiles, chosen_places):
        block = block_from + unit
        query = query_rows(unit)
        rows = slice(unit * BLK, (unit + 1) * BLK)
        stat = 2 * 8 * unit
        acc = sums = None
        if first:
            own = tile_rows(cfg["own_tile"] + block)
            scores = dot(kx[own, :], query, 1, 1)
            key_at = lax.broadcasted_iota(jnp.int32, scores.shape, 0)
            query_at = lax.broadcasted_iota(jnp.int32, scores.shape, 1) % BLK
            scores = jnp.where(key_at <= query_at, scores, NEG) * factor
            peak = jnp.broadcast_to(jnp.max(scores, axis=0, keepdims=True), (8, width))
            weights = jnp.exp2(scores - peak[:1]).astype(BF16)
            sums = sublane_sums(weights.astype(F32))
            acc = dot(vx[own, :], weights, 0, 0)
        else:
            acc_in, stat_in = state_refs[0]
            sums = stat_in[stat : stat + 8, :]
            peak = stat_in[stat + 8 : stat + 16, :]
        base = peak[:1]
        if sum(tiles):
            keys = jnp.concatenate(
                [
                    jnp.concatenate([kv[: n * BLK, :LANES], mark[: n * BLK, :]], axis=1)
                    for n, (kv, mark) in zip(tiles, vert_refs)
                    if n
                ],
                axis=0,
            )
            values = jnp.concatenate(
                [kv[: n * BLK, LANES:] for n, (kv, _) in zip(tiles, vert_refs) if n], axis=0
            )
            weights = jnp.exp2(dot(keys, marked(query, block), 1, 1) * factor - base).astype(BF16)
            sums = sums + sublane_sums(weights.astype(F32))
            more = dot(values, weights, 0, 0)
            acc = more if acc is None else acc + more
        if chosen_places:
            chosen = [slash_tile(block, place) for place in chosen_places]
            keys = jnp.concatenate([kx[tile_rows(index), :] for index, _ in chosen], axis=0)
            values = jnp.concatenate([vx[tile_rows(index), :] for index, _ in chosen], axis=0)
            scores = dot(keys, query, 1, 1)
            parts = []
            for place, (_, bias) in enumerate(chosen):
                weights = jnp.exp2(
                    scores[place * BLK : (place + 1) * BLK, :] * factor + (bias - base)
                ).astype(BF16)
                sums = sums + sublane_sums(weights.astype(F32))
                parts.append(weights)
            more = dot(values, jnp.concatenate(parts, axis=0), 0, 0)
            acc = more if acc is None else acc + more
        if not first:
            acc = acc_in[rows, :] + acc
        if last:
            return finish(unit, acc, sums, peak)
        out_a[rows, :] = acc
        out_b[stat : stat + 8, :] = sums
        out_b[stat + 8 : stat + 16, :] = peak
        return None

    def redo(unit):
        block = block_from + unit
        query = query_rows(unit)
        copies = []
        row0 = 0
        for place, (kv, mark) in enumerate(spare_refs):
            part = pl.ds(row0, kv.shape[0])
            copies.append(pltpu.make_async_copy(kv, redo_k.at[part, :], redo_sems.at[2 * place]))
            copies.append(
                pltpu.make_async_copy(mark, redo_e.at[part, :], redo_sems.at[2 * place + 1])
            )
            row0 += kv.shape[0]
        for copy in copies:
            copy.start()
        for copy in copies:
            copy.wait()
        if cfg["packs"]:
            redo_k[row0 : row0 + pack_ref.shape[0], :] = pack_ref[...]
            redo_e[row0 : row0 + pack_ref.shape[0], :] = vert_refs[0][1][...]
        redo_acc[...] = jnp.zeros_like(redo_acc)
        redo_stat[0:8, :] = jnp.zeros((8, width), F32)
        redo_stat[8:16, :] = jnp.full((8, width), NEG, F32)

        def merge(scores, values):
            peak = redo_stat[8:16, :]
            high = jnp.maximum(peak, jnp.max(scores, axis=0, keepdims=True))
            weights = jnp.where(scores > 1e-3 * NEG, jnp.exp2(scores - high[:1]), 0.0).astype(BF16)
            shrink = jnp.exp2(peak - high)
            redo_stat[0:8, :] = redo_stat[0:8, :] * shrink + sublane_sums(weights.astype(F32))
            redo_stat[8:16, :] = high
            redo_acc[...] = redo_acc[...] * shrink[:1] + dot(values, weights, 0, 0)

        def slash_step(place, carry):
            index, bias = slash_tile(block, place)
            scores = dot(kx[tile_rows(index), :], query, 1, 1) * factor + bias
            key_at = lax.broadcasted_iota(jnp.int32, scores.shape, 0)
            query_at = lax.broadcasted_iota(jnp.int32, scores.shape, 1) % BLK
            reach = jnp.where(offsets[head_index, place] > 0, BLK, 0)
            merge(jnp.where(key_at <= query_at + reach, scores, NEG), vx[tile_rows(index), :])
            return carry

        def vert_step(tile, carry):
            here = tile_rows(tile)
            keys = jnp.concatenate([redo_k[here, :LANES], redo_e[here, :]], axis=1)
            merge(dot(keys, marked(query, block), 1, 1) * factor, redo_k[here, LANES:])
            return carry

        lax.fori_loop(0, nslash, slash_step, 0)
        lax.fori_loop(0, redo_k.shape[0] // BLK, vert_step, 0)
        finish(unit, redo_acc[...], redo_stat[0:8, :], redo_stat[8:16, :])

    def redo_one(unit, carry):
        redo(unit)
        return carry

    def whole_step(tiles, chosen_places):
        totals = [one_unit(unit, tiles, chosen_places) for unit in range(per_step)]
        if last:
            worst = jnp.zeros((1, width), F32)
            for total in totals:
                worst = jnp.maximum(worst, jnp.where(total < LIMIT, 0.0, 1.0))
            redo_flag[0] = jnp.where(jnp.max(worst) > 0.0, 1, 0)

    groups = cfg["groups"]
    limited = [g for g, n in enumerate(groups) if n > 2 and cfg["counted"][g] is not None]
    few = [2 if g in limited else n for g, n in enumerate(groups)]
    fits = functools.reduce(
        jnp.logical_and, [counts[cfg["counted"][g]] <= 2 * BLK for g in limited], step >= 0
    )
    every = list(range(1, nslash))

    def sized_step(wanted, places):
        if limited:

            @pl.when(jnp.logical_and(fits, wanted))
            def _():
                whole_step(few, places)

        @pl.when(jnp.logical_and(jnp.logical_not(fits), wanted) if limited else wanted)
        def _():
            whole_step(groups, places)

    if not cfg["ahead"]:
        sized_step(step >= 0, [])
        return
    share = cfg["steps"] // len(cfg["ahead"])
    if limited:
        fits = jnp.logical_and(counts[1] <= 2 * BLK, counts[2] <= 2 * BLK)
    for part, ahead in enumerate(cfg["ahead"]):
        within = (step >= part * share) & (step < (part + 1) * share)
        early = offsets[head_index, ahead] <= cfg["tok_rows"] + part * share * per_step * BLK
        early = jnp.logical_and(early, fits)

        @pl.when(jnp.logical_and(within, early))
        def _():
            whole_step(few, every[ahead:] if last else every[:ahead])

        @pl.when(jnp.logical_and(within, jnp.logical_not(early)))
        def _():
            whole_step(groups, every if last else [])

    if last:

        @pl.when(redo_flag[0] > 0)
        def _():
            lax.fori_loop(0, per_step, redo_one, 0)


def stage(
    offsets, counts, queries, states, verts, counted, sources, spare, *,
    blocks, first=False, last=False, ahead=(), own_tile=0, tiles=0, pack_row0=None,
    per_step=4, cost=6,
):
    rows, columns = queries.shape
    heads = columns // LANES
    width = heads * BLK
    step_from = blocks[0] // per_step
    steps = (blocks[1] - blocks[0]) // per_step
    packs = pack_row0 is not None
    cfg = dict(
        per_step=per_step,
        nblocks=rows // BLK,
        tok_rows=rows,
        step_from=step_from,
        steps=steps,
        ahead=ahead,
        factor=1.0 / (math.sqrt(LANES) * LN2),
        first=first,
        last=last,
        states=len(states),
        own_tile=own_tile,
        groups=[mark.shape[0] // BLK for _, mark in verts],
        counted=counted,
        sources=[(row0, mine.shape[0], fixed) for row0, fixed, mine, _ in sources],
        spares=len(spare),
        packs=packs,
        pack_row0=pack_row0,
    )

    def moving(block_rows, from_step=0, count=steps):
        return pl.BlockSpec(
            (block_rows * per_step, width),
            lambda step, *_: (jnp.clip(step - from_step, 0, count - 1), 0),
        )

    def whole(array):
        return pl.BlockSpec(array.shape, lambda step, *_: (0, 0))

    anywhere = pl.BlockSpec(memory_space=pl.ANY)
    operands = [queries]
    specs = [pl.BlockSpec((BLK * per_step, columns), lambda s, *_: (s + step_from, 0))]
    for (array_a, array_b), from_block in states:
        count = array_a.shape[0] // (BLK * per_step)
        operands += [array_a, array_b]
        from_step = from_block // per_step - step_from
        specs += [moving(BLK, from_step, count), moving(16, from_step, count)]
    for pair in verts:
        operands += list(pair)
        specs += [whole(array) for array in pair]
    for _, _, mine, other in sources:
        operands += [mine, other]
        specs += [anywhere, anywhere]
    for pair in spare:
        operands += list(pair)
        specs += [anywhere, anywhere]
    scratch = []
    if sources:
        scratch += [
            pltpu.VMEM((tiles * BLK, LANES), BF16),
            pltpu.VMEM((tiles * BLK, LANES), BF16),
            pltpu.SemaphoreType.DMA((2 * len(sources),)),
        ]
    slot_pad = verts[0][1].shape[0] if verts else 0
    if packs:
        scratch += [pltpu.VMEM((slot_pad, 2 * LANES), BF16)]
    if last:
        out_shape = [
            jax.ShapeDtypeStruct((rows, columns), BF16),
            jax.ShapeDtypeStruct((heads, rows), F32),
        ]
        out_specs = [
            pl.BlockSpec((BLK * per_step, columns), lambda s, *_: (s, 0)),
            pl.BlockSpec((heads, BLK * per_step), lambda s, *_: (0, s)),
        ]
        spare_rows = sum(kv.shape[0] for kv, _ in spare) + slot_pad * packs
        scratch += [
            pltpu.VMEM((spare_rows, 2 * LANES), BF16),
            pltpu.VMEM((spare_rows, LANES), BF16),
            pltpu.VMEM((BLK, width), F32),
            pltpu.VMEM((16, width), F32),
            pltpu.SemaphoreType.DMA((2 * len(spare),)),
            pltpu.SMEM((1,), jnp.int32),
        ]
    else:
        out_shape = [
            jax.ShapeDtypeStruct((steps * per_step * BLK, width), F32),
            jax.ShapeDtypeStruct((steps * per_step * 16, width), F32),
        ]
        out_specs = [moving(BLK), moving(16)]
        if packs:
            out_shape.append(jax.ShapeDtypeStruct((slot_pad, 2 * LANES), BF16))
            out_specs.append(pl.BlockSpec((slot_pad, 2 * LANES), lambda s, *_: (0, 0)))
    return pl.pallas_call(
        functools.partial(stage_kernel, cfg),
        grid_spec=pltpu.PrefetchScalarGridSpec(
            num_scalar_prefetch=2,
            grid=(steps,),
            in_specs=specs,
            out_specs=out_specs,
            scratch_shapes=scratch,
        ),
        out_shape=out_shape,
        compiler_params=pltpu.CompilerParams(vmem_limit_bytes=VMEM_BYTES),
        cost_estimate=pl.CostEstimate(
            flops=cost * 1000000000, bytes_accessed=1 << 20, transcendentals=0
        ),
        name="attend_stage",
    )(offsets, counts, *operands)


def body(queries, key_rows, value_rows, vertical_columns, slash_offsets):
    seq_count = lax.axis_size("seq")
    core = lax.axis_index("rep")
    tok_rows = queries.shape[0]
    nblocks = tok_rows // BLK
    radius = (SPAN + nblocks - 2) // nblocks
    slot_count = 3 * vertical_columns.shape[1] // (2 * seq_count)
    slot_pad = -(-slot_count // BLK) * BLK
    near = radius + 1

    payload = jnp.where(core == 0, key_rows, value_rows)
    everything = (0, nblocks)
    moved = shifted(payload, "seq", 1)

    prepared = prep(
        slash_offsets, vertical_columns, key_rows, value_rows, seq_count, near, slot_pad
    )
    marks, places = prepared[: near + 1], prepared[near + 1 : -2]
    own_pack, counts = prepared[-2:]
    run = functools.partial(stage, slash_offsets, counts, queries, blocks=everything)

    own_verts = (own_pack, marks[0])
    own_row0 = radius * tok_rows
    far_moved = []
    if seq_count > near:
        far_payload = jnp.where(core == 0, own_pack[:, :LANES], own_pack[:, LANES:])
        far_moved = [
            shifted(far_payload, "seq", distance) for distance in range(near, seq_count)
        ]
    state = run(
        [], [own_verts], [0], [(0, True, key_rows, value_rows)], [], first=True, tiles=nblocks
    )
    moved, state, far_moved = after(moved, state, far_moved)
    moved2 = shifted(moved, "seq", 1)
    hop1 = (moved, swapped(moved))

    far_verts = []
    if far_moved:
        rows = []
        for mine in far_moved:
            other = swapped(mine)
            rows.append(
                jnp.where(
                    core == 0,
                    jnp.concatenate([mine, other], axis=1),
                    jnp.concatenate([other, mine], axis=1),
                )
            )
        far_verts = [(jnp.concatenate(rows, axis=0) if len(rows) > 1 else rows[0], marks[near])]

    *state, hop_pack = run(
        [(state, 0)], [(places[1], marks[1])] + far_verts, [1] + [None] * len(far_verts),
        [(0, False) + hop1, (tok_rows, True, key_rows, value_rows)], [], ahead=EARLY,
        own_tile=nblocks, tiles=2 * nblocks, pack_row0=0,
    )
    moved2, state = after(moved2, state)
    return tuple(
        run(
            [(state, 0)], [(places[2], marks[2])], [2],
            [
                (0, False, moved2, swapped(moved2)),
                (own_row0 - tok_rows, False) + hop1,
                (own_row0, True, key_rows, value_rows),
            ],
            [own_verts, (hop_pack, marks[1])] + far_verts,
            last=True, ahead=EARLY, own_tile=radius * nblocks,
            tiles=(radius + 1) * nblocks, pack_row0=0,
        )
    )


def solution(mesh):
    placed = (
        P(("groups", "seq"), ("head", "rep")),
        P(("groups", "seq"), "head"),
        P(("groups", "seq"), "head"),
        P("groups", None),
        P("groups", None),
    )
    return jax.shard_map(
        body,
        mesh=mesh,
        in_specs=placed,
        out_specs=(P(("groups", "seq"), ("head", "rep")), P(("head", "rep"), ("groups", "seq"))),
        check_vma=False,
    )
```
